32 devices in a mesh: wide: 16 (over z, y, x), narrow: 2 (over core).
Axes of the slice: x: 2, y: 2, z: 4, core: 2. Of those that a mesh axis runs over, the one named last changes fastest.
Arguments:
- pixels: bfloat16 [32, 512, 1024], P(('wide', 'narrow')), may hold values from -6 to 6
- layout: int32 [32], P(('wide', 'narrow')), may hold values from 0 to 1
- noise_group: int32 [32], P(('wide', 'narrow')), may hold values from 0 to 15
- cond_embed: bfloat16 [32, 1024], P(('wide', 'narrow')), may hold values from -6 to 6
- text_embed: bfloat16 [32, 128, 4096], P(('wide', 'narrow')), may hold values from -6 to 6
- cotangent: bfloat16 [32, 512, 1024], P(('wide', 'narrow')), may hold values from -6 to 6
- gn_gain: bfloat16 [1024], P('narrow'), may hold values from 0.099609375 to 1.8984375
- gn_bias: bfloat16 [1024], P('narrow'), may hold values from -3 to 3
- conv_in: bfloat16 [9, 1024, 1024], P(None, 'narrow'), may hold values from -0.0625 to 0.0625
- film_weight: bfloat16 [1024, 2048], P('narrow'), may hold values from -0.1875 to 0.1875
- film_bias: bfloat16 [2048], P('narrow'), may hold values from -3 to 3
- conv_out: bfloat16 [9, 1024, 1024], P(None, 'narrow'), may hold values from -0.0625 to 0.0625
- ln_gain: bfloat16 [1024], P('narrow'), may hold values from 0.099609375 to 1.8984375
- qkv_weight: bfloat16 [1024, 3072], P('narrow'), may hold values from -0.1875 to 0.1875
- out_weight: bfloat16 [1024, 1024], P('narrow'), may hold values from -3 to 3
- text_weight: bfloat16 [4096, 2048], P('narrow'), may hold values from -0.09375 to 0.09375
Outputs:
- output: bfloat16 [32, 512, 1024], P(('wide', 'narrow'))
- input_grad: bfloat16 [32, 512, 1024], P(('wide', 'narrow'))
- grad_gn_gain: float32 [1024], P('narrow')
- grad_gn_bias: float32 [1024], P('narrow')
- grad_conv_in: float32 [9, 1024, 1024], P(None, 'narrow')
- grad_film_weight: float32 [1024, 2048], P('narrow')
- grad_film_bias: float32 [2048], P('narrow')
- grad_conv_out: float32 [9, 1024, 1024], P(None, 'narrow')
- grad_ln_gain: float32 [1024], P('narrow')
- grad_qkv_weight: float32 [1024, 3072], P('narrow')
- grad_out_weight: float32 [1024, 1024], P('narrow')
- grad_text_weight: float32 [4096, 2048], P('narrow')
The draws below stay inside these ranges and needn't reach their ends.
Inputs may be any that keep to these rules, and one draw needn't show every extreme that they name: `layout`: 1: the image's 16 x 32 pixels form one map; 0: its four quarters are four separate maps.
All inputs are finite; a program needn't handle non-finite values.
Results may differ from the reference program's by a relative error of at most 0.024.
Values may be sent and summed in bfloat16 or wider, within the bound.
A program may use at most 384 MiB of HBM per device.

```python
import jax
import jax.numpy as jnp
from jax import lax

C = 1024
NORM_GROUPS = 32
HEADS = 8
TEXT_D = 4096
TEXT_LEN = 128
COND = 1024
MAP_H = 16
MAP_W = 32
HEAD_DIM = 128
PIXELS = 512
IMAGES = 32
NGROUPS = 16


def plant(drawn, own_key, smallest, top_value):
    extent = drawn.shape
    spot = [jax.random.randint(jax.random.fold_in(own_key, axis), (), 0, extent[axis]) for axis in range(len(extent))]
    drawn = drawn.at[tuple(spot)].set(smallest)
    longest = extent.index(max(extent))
    spot[longest] = (spot[longest] + 1) % extent[longest]
    return drawn.at[tuple(spot)].set(top_value)


def shard_levels(own_key, extent, cuts, least, largest):
    def one(dim, parts):
        heights = jax.random.uniform(jax.random.fold_in(jax.random.fold_in(own_key, 6), dim), (parts,), jnp.float32, least / len(cuts), largest / len(cuts))
        return jnp.repeat(jnp.exp(heights), extent[dim] // parts).reshape((-1,) + (1,) * (len(extent) - dim - 1))

    factor_of = one(*cuts[0])
    for cut in cuts[1:]:
        factor_of = factor_of * one(*cut)
    return factor_of


def gaussian(own_key, shape, deviation, most, shards=(), kind=jnp.bfloat16):
    gain = shard_levels(own_key, shape, shards, -0.22, 0.18) if shards else 1.0
    array = jax.random.normal(own_key, shape, jnp.float32) * deviation * gain
    return jnp.minimum(jnp.maximum(array, -most), most).astype(kind)


def setup_inputs(seed: int = 0) -> dict:
    streams_of = jax.random.split(jax.random.key(seed), 17)
    pixels = gaussian(streams_of[0], (IMAGES, PIXELS, C), 1.0, 6.0, ((0, 32),))
    layout = plant(jax.random.randint(streams_of[1], (IMAGES,), 0, 2), jax.random.fold_in(streams_of[1], 1), 0, 1).astype(jnp.int32)
    noise_group = plant(jax.random.randint(streams_of[2], (IMAGES,), 0, NGROUPS), jax.random.fold_in(streams_of[2], 1), 0, NGROUPS - 1).astype(jnp.int32)
    cond_embed = gaussian(streams_of[3], (IMAGES, COND), 1.0, 6.0, ((0, 32),))
    text_embed = gaussian(streams_of[4], (IMAGES, TEXT_LEN, TEXT_D), 1.0, 6.0, ((0, 32),))
    cotangent = gaussian(streams_of[5], (IMAGES, PIXELS, C), 1.0, 6.0, ((0, 32),))
    gn_gain = jnp.clip(1.0 + 0.18 * jax.random.normal(streams_of[6], (C,), jnp.float32), 0.099609375, 1.8984375).astype(jnp.bfloat16)
    gn_bias = gaussian(streams_of[7], (C,), 0.5, 3.0, ((0, 2),))
    conv_in = gaussian(streams_of[8], (9, C, C), (9 * C) ** -0.5, 0.0625, ((1, 2),))
    film_weight = gaussian(streams_of[9], (COND, 2 * C), COND ** -0.5, 0.1875, ((0, 2),))
    film_bias = gaussian(streams_of[10], (2 * C,), 0.5, 3.0, ((0, 2),))
    conv_out = gaussian(streams_of[11], (9, C, C), (9 * C) ** -0.5, 0.0625, ((1, 2),))
    ln_gain = jnp.clip(1.0 + 0.18 * jax.random.normal(streams_of[12], (C,), jnp.float32), 0.099609375, 1.8984375).astype(jnp.bfloat16)
    qkv_weight = gaussian(streams_of[13], (C, 3 * C), C ** -0.5, 0.1875, ((0, 2),))
    out_weight = gaussian(streams_of[14], (C, C), (max(C // 256, 1)) ** -0.5, 3.0, ((0, 2),))
    text_weight = gaussian(streams_of[15], (TEXT_D, 2 * C), TEXT_D ** -0.5, 0.09375, ((0, 2),))
    return dict(pixels=pixels, layout=layout, noise_group=noise_group, cond_embed=cond_embed, text_embed=text_embed, cotangent=cotangent, gn_gain=gn_gain, gn_bias=gn_bias, conv_in=conv_in, film_weight=film_weight, film_bias=film_bias, conv_out=conv_out, ln_gain=ln_gain, qkv_weight=qkv_weight, out_weight=out_weight, text_weight=text_weight)


highest = lax.Precision.HIGHEST
epsilon = 1e-05
inv_root_two = 0.7071067811865476
masked_score = -1e+30

@jax.custom_vjp
def low(v):
    return lax.optimization_barrier(v.astype(jnp.bfloat16)).astype(jnp.float32)

@jax.custom_vjp
def low_back(v):
    return v

def low_keep(v):
    return (low(v), None)

def low_pass(kept, grad):
    return (grad,)

def back_keep(v):
    return (v, None)

def back_low(kept, grad):
    return (low(grad),)
low.defvjp(low_keep, low_pass)
low_back.defvjp(back_keep, back_low)

def region_ids_of(layout_value):
    position = jnp.arange(MAP_H * MAP_W, dtype=jnp.int32)
    quarter = 2 * (position // MAP_W >= MAP_H // 2).astype(jnp.int32) + (position % MAP_W >= MAP_W // 2).astype(jnp.int32)
    return jnp.where(layout_value == 1, jnp.zeros_like(quarter), quarter)

def tap_validity(region_ids):
    code_grid = region_ids.reshape(MAP_H, MAP_W)
    padded = jnp.pad(code_grid, 1, constant_values=-1)
    found = []
    for row_step in (-1, 0, 1):
        for col_step in (-1, 0, 1):
            neighbour = padded[1 + row_step:1 + row_step + MAP_H, 1 + col_step:1 + col_step + MAP_W]
            found.append((neighbour == code_grid).reshape(-1))
    return jnp.stack(found)

def unfold(values, tap_valid):
    channels = values.shape[-1]
    padded = jnp.pad(values.reshape(MAP_H, MAP_W, channels), ((1, 1), (1, 1), (0, 0)))
    pieces = []
    tap_index = 0
    for row_step in (-1, 0, 1):
        for col_step in (-1, 0, 1):
            neighbour = padded[1 + row_step:1 + row_step + MAP_H, 1 + col_step:1 + col_step + MAP_W].reshape(MAP_H * MAP_W, channels)
            pieces.append(jnp.where(tap_valid[tap_index][:, None], neighbour, jnp.zeros_like(neighbour)))
            tap_index += 1
    return jnp.concatenate(pieces, axis=1)

def group_norm(values, members):
    pixel_count, channels = values.shape
    grouped = values.reshape(pixel_count, NORM_GROUPS, channels // NORM_GROUPS)
    counts = jnp.maximum(lax.optimization_barrier(jnp.sum(members, axis=0)) * (channels // NORM_GROUPS), 1.0)
    region_sums = jnp.einsum('pr,pg->rg', members, lax.optimization_barrier(jnp.sum(grouped, axis=2)), precision=highest)
    pixel_means = jnp.einsum('pr,rg->pg', members, region_sums / counts[:, None], precision=highest)
    centred = grouped - pixel_means[:, :, None]
    squares = jnp.einsum('pr,pg->rg', members, lax.optimization_barrier(jnp.sum(centred * centred, axis=2)), precision=highest)
    spreads = jnp.einsum('pr,rg->pg', members, lax.rsqrt(squares / counts[:, None] + epsilon), precision=highest)
    return (centred * spreads[:, :, None]).reshape(pixel_count, channels)

def layer_norm(field, gain_in):
    centre = field - lax.optimization_barrier(jnp.mean(field, axis=1, keepdims=True))
    return centre * lax.rsqrt(lax.optimization_barrier(jnp.mean(centre * centre, axis=1, keepdims=True)) + epsilon) * gain_in

def image_forward(pixels_one, region_ids, cond_one, text_one, params):
    gain_in, bias_in, conv_first, film_full, film_bias_full, conv_second, ln_full, qkv_full, out_full, text_full = params
    members = (region_ids[:, None] == jnp.arange(4, dtype=jnp.int32)[None, :]).astype(jnp.float32)
    tap_valid = tap_validity(region_ids)
    first_act = jax.nn.silu(group_norm(pixels_one, members) * gain_in + bias_in)
    hidden_one = low_back(jnp.dot(unfold(low(first_act), tap_valid), conv_first.reshape(9 * C, C), precision=highest))
    condition = low(jax.nn.silu(cond_one))
    film_out = low_back(jnp.dot(condition, film_full, precision=highest) + film_bias_full)
    second_act = jax.nn.silu(group_norm(hidden_one, members) * (1.0 + film_out[:C]) + film_out[C:])
    hidden_two = low_back(jnp.dot(unfold(low(second_act), tap_valid), conv_second.reshape(9 * C, C), precision=highest))
    joined = (pixels_one + hidden_two) * inv_root_two
    normed_low = low(layer_norm(joined, ln_full))
    triple = low(low_back(jnp.dot(normed_low, qkv_full, precision=highest)))
    text_pair = low(low_back(jnp.dot(text_one, text_full, precision=highest)))
    queries = triple[:, :C].reshape(PIXELS, HEADS, HEAD_DIM)
    key_rows = jnp.concatenate([triple[:, C:2 * C], text_pair[:, :C]], axis=0).reshape(PIXELS + TEXT_LEN, HEADS, HEAD_DIM)
    value_rows = jnp.concatenate([triple[:, 2 * C:], text_pair[:, C:]], axis=0).reshape(PIXELS + TEXT_LEN, HEADS, HEAD_DIM)
    allowed = jnp.concatenate([region_ids[:, None] == region_ids[None, :], jnp.ones((PIXELS, TEXT_LEN), dtype=jnp.bool_)], axis=1)
    scores = low_back(jnp.einsum('phd,jhd->hpj', queries, key_rows, precision=highest) * HEAD_DIM ** (-0.5))
    masked = jnp.where(allowed[None], scores, masked_score)
    exponent = jnp.exp(masked - lax.optimization_barrier(jnp.max(masked, axis=2, keepdims=True)))
    attn_probs = exponent / lax.optimization_barrier(jnp.sum(exponent, axis=2, keepdims=True))
    mixed = low(low_back(jnp.einsum('hpj,jhd->phd', low(attn_probs), value_rows, precision=highest).reshape(PIXELS, C)))
    return joined + jnp.dot(mixed, out_full, precision=highest)

def reference(pixels, layout, noise_group, cond_embed, text_embed, cotangent, gn_gain, gn_bias, conv_in, film_weight, film_bias, conv_out, ln_gain, qkv_weight, out_weight, text_weight):
    params = tuple((weight_arg.astype(jnp.float32) for weight_arg in (gn_gain, gn_bias, conv_in, film_weight, film_bias, conv_out, ln_gain, qkv_weight, out_weight, text_weight)))
    onehot_groups = (noise_group[:, None] == jnp.arange(NGROUPS, dtype=jnp.int32)[None, :]).astype(jnp.float32)
    counts = lax.optimization_barrier(jnp.sum(onehot_groups, axis=0))
    image_weights = 1.0 / (NGROUPS * lax.optimization_barrier(jnp.sum(onehot_groups * counts[None, :], axis=1)))

    def step_image(running, scanned):
        pixels_one, layout_one, cond_one, text_one, cot_one, weight_one = scanned
        region_ids = region_ids_of(layout_one)

        def forward(pixels_in, params_in):
            return image_forward(pixels_in, region_ids, cond_one.astype(jnp.float32), text_one.astype(jnp.float32), params_in)
        output_one, pullback = jax.vjp(forward, pixels_one.astype(jnp.float32), params)
        grad_in, grad_params = pullback(cot_one.astype(jnp.float32))
        running = jax.tree.map(lambda summed, fresh: summed + weight_one * fresh, running, grad_params)
        return (running, (output_one.astype(jnp.bfloat16), grad_in.astype(jnp.bfloat16)))
    zero_grads = jax.tree.map(jnp.zeros_like, params)
    totals, (output, input_grad) = lax.scan(step_image, zero_grads, (pixels, layout, cond_embed, text_embed, cotangent, image_weights))
    return (output, input_grad, totals[0], totals[1], totals[2], totals[3], totals[4], totals[5], totals[6], totals[7], totals[8], totals[9])
```

```python
import functools

import jax
import jax.numpy as jnp
from jax import lax
from jax.experimental import pallas as pl
from jax.experimental.pallas import tpu as pltpu
from jax.sharding import PartitionSpec as P

NORM_GROUPS = 32
HEADS = 8
TEXT_LEN = 128
MAP_H = 16
MAP_W = 32


highest = lax.Precision.HIGHEST
epsilon = 1e-05
inv_root_two = 0.7071067811865476
masked_score = -1e30


def region_ids_of(layout_value):
    position = jnp.arange(MAP_H * MAP_W, dtype=jnp.int32)
    quarter = 2 * (position // MAP_W >= MAP_H // 2).astype(jnp.int32) + (
        position % MAP_W >= MAP_W // 2
    ).astype(jnp.int32)
    return jnp.where(layout_value == 1, jnp.zeros_like(quarter), quarter)


def tap_validity(region_ids):
    code_grid = region_ids.reshape(MAP_H, MAP_W)
    padded = jnp.pad(code_grid, 1, constant_values=-1)
    found = []
    for row_step in (-1, 0, 1):
        for col_step in (-1, 0, 1):
            neighbour = padded[
                1 + row_step : 1 + row_step + MAP_H, 1 + col_step : 1 + col_step + MAP_W
            ]
            found.append((neighbour == code_grid).reshape(-1))
    return jnp.stack(found)


def unfold(values, tap_valid):
    channels = values.shape[-1]
    padded = jnp.pad(values.reshape(MAP_H, MAP_W, channels), ((1, 1), (1, 1), (0, 0)))
    pieces = []
    tap_index = 0
    for row_step in (-1, 0, 1):
        for col_step in (-1, 0, 1):
            neighbour = padded[
                1 + row_step : 1 + row_step + MAP_H, 1 + col_step : 1 + col_step + MAP_W
            ].reshape(MAP_H * MAP_W, channels)
            pieces.append(
                jnp.where(tap_valid[tap_index][:, None], neighbour, jnp.zeros_like(neighbour))
            )
            tap_index += 1
    return jnp.concatenate(pieces, axis=1)


def fold_back(grad_cols, tap_valid):
    channels = grad_cols.shape[1] // 9
    start_point = jnp.zeros((grad_cols.shape[0], channels), jnp.float32)
    unfolded, pullback = jax.vjp(lambda field: unfold(field, tap_valid), start_point)
    return pullback(grad_cols)[0]


def group_norm(values, members):
    pixel_count, channels = values.shape
    grouped = values.reshape(pixel_count, NORM_GROUPS, channels // NORM_GROUPS)
    counts = jnp.maximum(jnp.sum(members, axis=0) * (channels // NORM_GROUPS), 1.0)
    region_sums = jnp.einsum("pr,pg->rg", members, jnp.sum(grouped, axis=2), precision=highest)
    pixel_means = jnp.einsum("pr,rg->pg", members, region_sums / counts[:, None], precision=highest)
    centred = grouped - pixel_means[:, :, None]
    squares = jnp.einsum(
        "pr,pg->rg", members, jnp.sum(centred * centred, axis=2), precision=highest
    )
    spreads = jnp.einsum(
        "pr,rg->pg", members, lax.rsqrt(squares / counts[:, None] + epsilon), precision=highest
    )
    return (centred * spreads[:, :, None]).reshape(pixel_count, channels)


def layer_norm(field, gain_in):
    centre = field - jnp.mean(field, axis=1, keepdims=True)
    return centre * lax.rsqrt(jnp.mean(centre * centre, axis=1, keepdims=True) + epsilon) * gain_in


def first_block(field, gain_in, bias_in, members):
    return jax.nn.silu(group_norm(field, members) * gain_in + bias_in)


def mid_block(hidden_in, film_in, members):
    channels = hidden_in.shape[1]
    return jax.nn.silu(
        group_norm(hidden_in, members) * (1.0 + film_in[:channels]) + film_in[channels:]
    )


def residual_front(field, members, tap_valid, condition, weights_full):
    gain_full, bias_full, conv_first, film_full, film_bias_full, conv_second = weights_full
    channels = field.shape[1]
    first_act, first_back = jax.vjp(
        lambda field_in, gain_in, bias_in: first_block(field_in, gain_in, bias_in, members),
        field,
        gain_full.astype(jnp.float32),
        bias_full.astype(jnp.float32),
    )
    first_low = first_act.astype(jnp.bfloat16)
    first_cols = unfold(first_low, tap_valid)
    hidden_one = jnp.dot(
        first_cols, conv_first.reshape(-1, channels), preferred_element_type=jnp.float32
    )
    film_out = jnp.dot(
        condition, film_full, preferred_element_type=jnp.float32
    ) + film_bias_full.astype(jnp.float32)
    second_act, mid_back = jax.vjp(
        lambda hidden_in, film_in: mid_block(hidden_in, film_in, members), hidden_one, film_out
    )
    second_low = second_act.astype(jnp.bfloat16)
    second_cols = unfold(second_low, tap_valid)
    return (first_cols, second_cols, first_back, mid_back)


def allowed_keys(region_ids):
    same_region = region_ids[:, None] == region_ids[None, :]
    return jnp.concatenate(
        [same_region, jnp.ones((region_ids.shape[0], TEXT_LEN), dtype=jnp.bool_)], axis=1
    )


def attention_forward(joined, text_one, region_ids, attn_full):
    gain_full, qkv_full, out_full, text_full = attn_full
    pixel_count, channels = joined.shape
    head_dim = channels // HEADS
    score_scale = head_dim ** (-0.5)
    normed_low = layer_norm(joined, gain_full.astype(jnp.float32)).astype(jnp.bfloat16)
    triple = jnp.dot(normed_low, qkv_full, preferred_element_type=jnp.float32).astype(jnp.bfloat16)
    text_pair = jnp.dot(text_one, text_full, preferred_element_type=jnp.float32).astype(
        jnp.bfloat16
    )
    queries = triple[:, :channels].reshape(pixel_count, HEADS, head_dim)
    key_rows = jnp.concatenate(
        [triple[:, channels : 2 * channels], text_pair[:, :channels]], axis=0
    ).reshape(-1, HEADS, head_dim)
    value_rows = jnp.concatenate(
        [triple[:, 2 * channels :], text_pair[:, channels:]], axis=0
    ).reshape(-1, HEADS, head_dim)
    allowed = allowed_keys(region_ids)
    masked = jnp.where(
        allowed[None],
        jnp.einsum("phd,jhd->hpj", queries, key_rows, preferred_element_type=jnp.float32)
        * score_scale,
        masked_score,
    )
    row_peak = jnp.max(masked, axis=2, keepdims=True)
    exponent = jnp.exp(masked - row_peak)
    exp_total = jnp.sum(exponent, axis=2, keepdims=True)
    attn_probs = exponent / exp_total
    log_total = row_peak + jnp.log(exp_total)
    mixed = (
        jnp.einsum(
            "hpj,jhd->phd",
            attn_probs.astype(jnp.bfloat16),
            value_rows,
            preferred_element_type=jnp.float32,
        )
        .reshape(pixel_count, channels)
        .astype(jnp.bfloat16)
    )
    result = joined + jnp.dot(mixed, out_full, preferred_element_type=jnp.float32)
    return (result, (normed_low, queries, key_rows, value_rows, log_total, mixed, allowed))


def attention_backward(grad_result, joined, text_one, stored, attn_full):
    gain_full, qkv_full, out_full, text_full = attn_full
    normed_low, queries, key_rows, value_rows, log_total, mixed, allowed = stored
    pixel_count, channels = joined.shape
    head_dim = channels // HEADS
    score_scale = head_dim ** (-0.5)
    grad_mixed = (
        jnp.einsum("pd,cd->pc", grad_result, out_full, preferred_element_type=jnp.float32)
        .astype(jnp.bfloat16)
        .reshape(pixel_count, HEADS, head_dim)
    )
    masked = jnp.where(
        allowed[None],
        jnp.einsum("phd,jhd->hpj", queries, key_rows, preferred_element_type=jnp.float32)
        * score_scale,
        masked_score,
    )
    attn_probs = jnp.exp(masked - log_total)
    grad_probs = jnp.einsum(
        "phd,jhd->hpj", grad_mixed, value_rows, preferred_element_type=jnp.float32
    )
    grad_values = jnp.einsum(
        "hpj,phd->jhd",
        attn_probs.astype(jnp.bfloat16),
        grad_mixed,
        preferred_element_type=jnp.float32,
    )
    row_inner = jnp.sum(attn_probs * grad_probs, axis=2, keepdims=True)
    grad_scores = (attn_probs * (grad_probs - row_inner)).astype(jnp.bfloat16)
    grad_queries = (
        jnp.einsum("hpj,jhd->phd", grad_scores, key_rows, preferred_element_type=jnp.float32)
        * score_scale
    )
    grad_keys = (
        jnp.einsum("hpj,phd->jhd", grad_scores, queries, preferred_element_type=jnp.float32)
        * score_scale
    )
    grad_triple = jnp.concatenate(
        [
            grad_queries.reshape(pixel_count, channels),
            grad_keys[:pixel_count].reshape(pixel_count, channels),
            grad_values[:pixel_count].reshape(pixel_count, channels),
        ],
        axis=1,
    ).astype(jnp.bfloat16)
    grad_pair = jnp.concatenate(
        [
            grad_keys[pixel_count:].reshape(-1, channels),
            grad_values[pixel_count:].reshape(-1, channels),
        ],
        axis=1,
    ).astype(jnp.bfloat16)
    term_out = jnp.einsum("pc,pd->cd", mixed, grad_result, preferred_element_type=jnp.float32)
    term_qkv = jnp.einsum("pc,pk->ck", normed_low, grad_triple, preferred_element_type=jnp.float32)
    term_text = jnp.einsum("tc,tk->ck", text_one, grad_pair, preferred_element_type=jnp.float32)
    big_terms = (term_qkv, term_out, term_text)
    grad_normed = jnp.einsum("pk,ck->pc", grad_triple, qkv_full, preferred_element_type=jnp.float32)
    normed_value, norm_back = jax.vjp(layer_norm, joined, gain_full.astype(jnp.float32))
    grad_joined_norm, term_gain = norm_back(grad_normed)
    return (grad_result.astype(jnp.float32) + grad_joined_norm, term_gain, big_terms)


def every_wide_sum(parts):
    return (
        lax.psum(parts[0].astype(jnp.bfloat16), "wide").astype(jnp.float32),
        lax.psum(parts[1].astype(jnp.bfloat16), "wide").astype(jnp.float32),
        lax.psum(parts[2].astype(jnp.bfloat16), "wide").astype(jnp.float32),
        lax.psum(parts[3].astype(jnp.bfloat16), "wide").astype(jnp.float32),
        lax.psum(parts[4].astype(jnp.bfloat16), "wide").astype(jnp.float32),
        lax.psum(parts[5].astype(jnp.bfloat16), "wide").astype(jnp.float32),
        lax.psum(parts[6].astype(jnp.bfloat16), "wide").astype(jnp.float32),
        lax.psum(parts[7].astype(jnp.bfloat16), "wide").astype(jnp.float32),
        lax.psum(parts[8].astype(jnp.bfloat16), "wide").astype(jnp.float32),
        lax.psum(parts[9].astype(jnp.bfloat16), "wide").astype(jnp.float32),
    )


def plain_body(
    pixels,
    layout,
    noise_group,
    cond_embed,
    text_embed,
    cotangent,
    gn_gain,
    gn_bias,
    conv_in,
    film_weight,
    film_bias,
    conv_out,
    ln_gain,
    qkv_weight,
    out_weight,
    text_weight,
):
    group_total = lax.axis_size("wide")
    onehot_groups = (
        noise_group[:, None] == jnp.arange(group_total, dtype=jnp.int32)[None, :]
    ).astype(jnp.float32)
    counts = lax.psum(jnp.sum(onehot_groups, axis=0), ("wide", "narrow"))
    slot_weights = 1.0 / (group_total * jnp.sum(onehot_groups * counts[None, :], axis=1))
    res_full = (
        lax.all_gather(gn_gain, "narrow", axis=0, tiled=True),
        lax.all_gather(gn_bias, "narrow", axis=0, tiled=True),
        lax.all_gather(conv_in, "narrow", axis=1, tiled=True),
        lax.all_gather(film_weight, "narrow", axis=0, tiled=True),
        lax.all_gather(film_bias, "narrow", axis=0, tiled=True),
        lax.all_gather(conv_out, "narrow", axis=1, tiled=True),
    )
    attn_full = (
        lax.all_gather(ln_gain, "narrow", axis=0, tiled=True),
        lax.all_gather(qkv_weight, "narrow", axis=0, tiled=True),
        lax.all_gather(out_weight, "narrow", axis=0, tiled=True),
        lax.all_gather(text_weight, "narrow", axis=0, tiled=True),
    )
    channels = pixels.shape[2]
    slot_index = 0
    field = pixels[slot_index].astype(jnp.float32)
    region_ids = region_ids_of(layout[slot_index])
    members = (region_ids[:, None] == jnp.arange(4, dtype=jnp.int32)[None, :]).astype(jnp.float32)
    tap_valid = tap_validity(region_ids)
    condition = jax.nn.silu(cond_embed[slot_index].astype(jnp.float32)).astype(jnp.bfloat16)
    front = residual_front(field, members, tap_valid, condition, res_full)
    hidden_two = jnp.dot(
        front[1], res_full[5].reshape(-1, channels), preferred_element_type=jnp.float32
    )
    joined = (field + hidden_two) * inv_root_two
    result, stored = attention_forward(joined, text_embed[slot_index], region_ids, attn_full)
    outputs = [result.astype(jnp.bfloat16)]
    saved = [(field, members, tap_valid, condition, joined, stored)]
    attn_big = tuple((jnp.zeros(full_weight.shape, jnp.float32) for full_weight in attn_full[1:]))
    slot_index = 0
    field, members, tap_valid, condition, joined, stored = saved[slot_index]
    grad_joined, term_gain, big_terms = attention_backward(
        cotangent[slot_index], joined, text_embed[slot_index], stored, attn_full
    )
    joined_grads = [grad_joined]
    gain_sum = slot_weights[slot_index] * term_gain
    attn_big = tuple((slot_weights[slot_index] * fresh for fresh in big_terms))
    grad_ln_gain, grad_qkv_weight, grad_out_weight, grad_text_weight = (
        lax.psum_scatter(
            gain_sum.astype(jnp.bfloat16), "narrow", scatter_dimension=0, tiled=True
        ).astype(jnp.float32),
        lax.psum_scatter(
            attn_big[0].astype(jnp.bfloat16), "narrow", scatter_dimension=0, tiled=True
        ).astype(jnp.float32),
        lax.psum_scatter(
            attn_big[1].astype(jnp.bfloat16), "narrow", scatter_dimension=0, tiled=True
        ).astype(jnp.float32),
        lax.psum_scatter(
            attn_big[2].astype(jnp.bfloat16), "narrow", scatter_dimension=0, tiled=True
        ).astype(jnp.float32),
    )
    res_back = (
        lax.all_gather(gn_gain, "narrow", axis=0, tiled=True),
        lax.all_gather(gn_bias, "narrow", axis=0, tiled=True),
        lax.all_gather(conv_in, "narrow", axis=1, tiled=True),
        lax.all_gather(film_weight, "narrow", axis=0, tiled=True),
        lax.all_gather(film_bias, "narrow", axis=0, tiled=True),
        lax.all_gather(conv_out, "narrow", axis=1, tiled=True),
    )
    conv_first = res_back[2].reshape(-1, channels)
    conv_second = res_back[5].reshape(-1, channels)
    small_sums = (
        jnp.zeros(res_back[0].shape, jnp.float32),
        jnp.zeros(res_back[1].shape, jnp.float32),
        jnp.zeros(res_back[4].shape, jnp.float32),
    )
    res_big = (
        jnp.zeros(res_back[2].shape, jnp.float32),
        jnp.zeros(res_back[3].shape, jnp.float32),
        jnp.zeros(res_back[5].shape, jnp.float32),
    )
    slot_index = 0
    field, members, tap_valid, condition, joined, stored = saved[slot_index]
    grad_joined = joined_grads[slot_index]
    first_cols, second_cols, first_back, mid_back = residual_front(
        field, members, tap_valid, condition, res_back
    )
    grad_two = (grad_joined * inv_root_two).astype(jnp.bfloat16)
    grad_second = fold_back(
        jnp.einsum("pc,kc->pk", grad_two, conv_second, preferred_element_type=jnp.float32),
        tap_valid,
    )
    grad_hidden, grad_film = mid_back(grad_second)
    grad_film_low = grad_film.astype(jnp.bfloat16)
    grad_one = grad_hidden.astype(jnp.bfloat16)
    grad_first = fold_back(
        jnp.einsum("pc,kc->pk", grad_one, conv_first, preferred_element_type=jnp.float32), tap_valid
    )
    grad_field, term_gain, term_bias = first_back(grad_first)
    input_grads = [(grad_joined * inv_root_two + grad_field).astype(jnp.bfloat16)]
    small_terms = (term_gain, term_bias, grad_film_low.astype(jnp.float32))
    small_sums = tuple((slot_weights[slot_index] * fresh for fresh in small_terms))
    term_conv_out = jnp.einsum(
        "pk,pc->kc", second_cols, grad_two, preferred_element_type=jnp.float32
    )
    term_film = jnp.einsum("k,c->kc", condition, grad_film_low, preferred_element_type=jnp.float32)
    term_conv_in = jnp.einsum("pk,pc->kc", first_cols, grad_one, preferred_element_type=jnp.float32)
    big_terms = (
        term_conv_in.reshape(res_back[2].shape),
        term_film,
        term_conv_out.reshape(res_back[5].shape),
    )
    res_big = tuple((slot_weights[slot_index] * fresh for fresh in big_terms))
    grad_gn_gain, grad_gn_bias, grad_conv_in, grad_film_weight, grad_film_bias, grad_conv_out = (
        lax.psum_scatter(
            small_sums[0].astype(jnp.bfloat16), "narrow", scatter_dimension=0, tiled=True
        ).astype(jnp.float32),
        lax.psum_scatter(
            small_sums[1].astype(jnp.bfloat16), "narrow", scatter_dimension=0, tiled=True
        ).astype(jnp.float32),
        lax.psum_scatter(
            res_big[0].astype(jnp.bfloat16), "narrow", scatter_dimension=1, tiled=True
        ).astype(jnp.float32),
        lax.psum_scatter(
            res_big[1].astype(jnp.bfloat16), "narrow", scatter_dimension=0, tiled=True
        ).astype(jnp.float32),
        lax.psum_scatter(
            small_sums[2].astype(jnp.bfloat16), "narrow", scatter_dimension=0, tiled=True
        ).astype(jnp.float32),
        lax.psum_scatter(
            res_big[2].astype(jnp.bfloat16), "narrow", scatter_dimension=1, tiled=True
        ).astype(jnp.float32),
    )
    (
        grad_gn_gain,
        grad_gn_bias,
        grad_conv_in,
        grad_film_weight,
        grad_film_bias,
        grad_conv_out,
        grad_ln_gain,
        grad_qkv_weight,
        grad_out_weight,
        grad_text_weight,
    ) = every_wide_sum(
        (
            grad_gn_gain,
            grad_gn_bias,
            grad_conv_in,
            grad_film_weight,
            grad_film_bias,
            grad_conv_out,
            grad_ln_gain,
            grad_qkv_weight,
            grad_out_weight,
            grad_text_weight,
        )
    )
    return (
        jnp.stack(outputs),
        jnp.stack(input_grads),
        grad_gn_gain,
        grad_gn_bias,
        grad_conv_in,
        grad_film_weight,
        grad_film_bias,
        grad_conv_out,
        grad_ln_gain,
        grad_qkv_weight,
        grad_out_weight,
        grad_text_weight,
    )


MESH = pl.DeviceIdType.MESH
LAG_B, LAG_C, LAG_D = 1, 2, 3

def comm_kernel(tx, qo, co, ci, tx_o, q_o, o_o, co_o, ci_o,
                held, total, cross, from_x, from_y, from_d,
                load_sem, s1s, s1r, s2s, s2r, s3s, s3r, xs, xr, ys, yr, d0s, d0r, d1s, d1r, out_sem):
    n = 30
    w = lax.axis_index("wide")
    c = lax.axis_index("narrow")
    p = w % 4
    z = w // 4
    wx = w + 1 - 2 * (w % 2)
    wy = w + 2 - 4 * ((w // 2) % 2)
    wz = w + 4 - 8 * (z % 2)
    wm = (3 - z) * 4 + p
    px = p + 1 - 2 * (p % 2)
    py = p + 2 - 4 * (p // 2)
    pd = 3 - p
    is_mid = (z == 1) | (z == 2)
    is_end = (z == 0) | (z == 3)

    bar = pltpu.get_barrier_semaphore()
    for t in (wx, wy, wz):
        pl.semaphore_signal(bar, inc=1, device_id=(t, c), device_id_type=MESH)

    @pl.when(is_mid)
    def _():
        pl.semaphore_signal(bar, inc=1, device_id=(wm, c), device_id_type=MESH)
        pl.semaphore_wait(bar, 4)

    @pl.when(is_end)
    def _():
        pl.semaphore_wait(bar, 3)

    def remote(src, dst, ss, rs, t):
        return pltpu.make_async_remote_copy(src_ref=src, dst_ref=dst, send_sem=ss, recv_sem=rs,
                                            device_id=(t, c), device_id_type=MESH)

    parts = ((tx, 0, 8), (qo, 8, 4), (co, 12, 9), (ci, 21, 9))

    for ref, base, count in parts:
        @pl.when(is_mid)
        def _(ref=ref, base=base, count=count):
            def go(i, _):
                pltpu.make_async_copy(ref.at[i], held.at[base + i], load_sem.at[base + i]).start()
                return 0
            lax.fori_loop(0, count, go, 0)

        @pl.when(is_end)
        def _(ref=ref, base=base, count=count):
            def go(i, _):
                remote(ref.at[i], total.at[base + i], s1s.at[base + i], s1r.at[base + i], wz).start()
                return 0
            lax.fori_loop(0, count, go, 0)

    def put_out(k, src, quarter, slot):
        col = pl.multiple_of(quarter * 256, 256)
        sem = out_sem.at[k, slot]
        @pl.when(k < 8)
        def _():
            i = k // 2
            j = k % 2
            pltpu.make_async_copy(src, tx_o.at[pl.ds(pl.multiple_of(i * 512, 512), 512), pl.ds(pl.multiple_of(j * 1024 + col, 256), 256)], sem).start()
        @pl.when((k >= 8) & (k < 11))
        def _():
            pltpu.make_async_copy(src, q_o.at[:, pl.ds(pl.multiple_of((k - 8) * 1024 + col, 256), 256)], sem).start()
        @pl.when(k == 11)
        def _():
            pltpu.make_async_copy(src, o_o.at[:, pl.ds(col, 256)], sem).start()
        @pl.when((k >= 12) & (k < 21))
        def _():
            pltpu.make_async_copy(src, co_o.at[k - 12, :, pl.ds(col, 256)], sem).start()
        @pl.when(k >= 21)
        def _():
            pltpu.make_async_copy(src, ci_o.at[k - 21, :, pl.ds(col, 256)], sem).start()

    def step(k, _):
        @pl.when(is_mid & (k < n))
        def _():
            pltpu.make_async_copy(co.at[0], held.at[k], load_sem.at[k]).wait()
            remote(total.at[k], total.at[k], s1s.at[k], s1r.at[k], wz).wait_recv()
            held[k] = (held[k].astype(jnp.float32) + total[k].astype(jnp.float32)).astype(jnp.bfloat16)
            remote(held.at[k], cross.at[k], s2s.at[k], s2r.at[k], wm).start()

        kb = k - LAG_B

        @pl.when((kb >= 0) & (kb < n))
        def _():
            @pl.when(is_mid)
            def _():
                remote(held.at[kb], cross.at[kb], s2s.at[kb], s2r.at[kb], wm).wait_recv()
                total[kb] = (held[kb].astype(jnp.float32) + cross[kb].astype(jnp.float32)).astype(jnp.bfloat16)
                remote(total.at[kb], total.at[kb], s3s.at[kb], s3r.at[kb], wz).start()
            @pl.when(is_end)
            def _():
                remote(total.at[kb], total.at[kb], s3s.at[kb], s3r.at[kb], wz).wait_recv()
            remote(total.at[kb], from_x.at[kb], xs.at[kb], xr.at[kb], wx).start()
            remote(total.at[kb], from_y.at[kb], ys.at[kb], yr.at[kb], wy).start()
            put_out(kb, total.at[kb], p, 0)

        kc = k - LAG_C

        @pl.when((kc >= 0) & (kc < n))
        def _():
            remote(total.at[kc], from_x.at[kc], xs.at[kc], xr.at[kc], wx).wait_recv()
            remote(total.at[kc], from_y.at[kc], ys.at[kc], yr.at[kc], wy).wait_recv()
            remote(from_y.at[kc, :256], from_d.at[kc, :256], d0s.at[kc], d0r.at[kc], wx).start()
            remote(from_x.at[kc, 256:], from_d.at[kc, 256:], d1s.at[kc], d1r.at[kc], wy).start()
            put_out(kc, from_x.at[kc], px, 1)
            put_out(kc, from_y.at[kc], py, 2)

        kd = k - LAG_D

        @pl.when(kd >= 0)
        def _():
            remote(from_y.at[kd, :256], from_d.at[kd, :256], d0s.at[kd], d0r.at[kd], wx).wait_recv()
            remote(from_x.at[kd, 256:], from_d.at[kd, 256:], d1s.at[kd], d1r.at[kd], wy).wait_recv()
            put_out(kd, from_d.at[kd], pd, 3)
        return 0

    lax.fori_loop(0, n + LAG_D, step, 0)

    def finish(k, _):
        @pl.when(is_end)
        def _():
            remote(co.at[0], total.at[k], s1s.at[k], s1r.at[k], wz).wait_send()
        @pl.when(is_mid)
        def _():
            remote(held.at[k], cross.at[k], s2s.at[k], s2r.at[k], wm).wait_send()
            remote(total.at[k], total.at[k], s3s.at[k], s3r.at[k], wz).wait_send()
        remote(total.at[k], from_x.at[k], xs.at[k], xr.at[k], wx).wait_send()
        remote(total.at[k], from_y.at[k], ys.at[k], yr.at[k], wy).wait_send()
        remote(from_y.at[k, :256], from_d.at[k, :256], d0s.at[k], d0r.at[k], wx).wait_send()
        remote(from_x.at[k, 256:], from_d.at[k, 256:], d1s.at[k], d1r.at[k], wy).wait_send()
        for slot in range(4):
            pltpu.make_async_copy(total.at[k], co_o.at[0, :, pl.ds(0, 256)], out_sem.at[k, slot]).wait()
        return 0

    lax.fori_loop(0, n, finish, 0)


def sum_and_gather(tx, qo, co, ci):
    n = 30
    bf = jnp.bfloat16
    any_spec = pl.BlockSpec(memory_space=pl.ANY)
    buf = pltpu.VMEM((n, 512, 256), bf)
    dma = pltpu.SemaphoreType.DMA((n,))
    return pl.pallas_call(
        comm_kernel,
        out_shape=(jax.ShapeDtypeStruct((2048, 2048), bf), jax.ShapeDtypeStruct((512, 3072), bf),
                   jax.ShapeDtypeStruct((512, 1024), bf), jax.ShapeDtypeStruct((9, 512, 1024), bf),
                   jax.ShapeDtypeStruct((9, 512, 1024), bf)),
        in_specs=[any_spec] * 4,
        out_specs=[any_spec] * 5,
        scratch_shapes=[buf] * 6 + [dma] * 15 + [pltpu.SemaphoreType.DMA((n, 4))],
        compiler_params=pltpu.CompilerParams(collective_id=0, has_side_effects=True, vmem_limit_bytes=60 << 20),
        name="sum_and_gather",
    )(tx, qo, co, ci)


CHUNK = 256
HALF_ROWS = 10 * MAP_W


def quadrants(values):
    grid = values.reshape(2, MAP_H // 2, 2, MAP_W // 2, values.shape[-1])
    return [grid[a, :, b] for a in range(2) for b in range(2)]


def rejoin(parts):
    channels = parts[0].shape[-1]
    top = jnp.concatenate(
        [part.reshape(MAP_H // 2, 1, MAP_W // 2, channels) for part in parts[:2]], axis=1
    )
    low = jnp.concatenate(
        [part.reshape(MAP_H // 2, 1, MAP_W // 2, channels) for part in parts[2:]], axis=1
    )
    return jnp.concatenate([top, low], axis=0).reshape(MAP_H * MAP_W, channels)


def region_mean(parts, single, block_ones):
    rows = jnp.concatenate(
        [jnp.sum(part, axis=(0, 1), keepdims=True).reshape(1, -1) for part in parts], axis=0
    )
    rows = jnp.concatenate([rows, rows], axis=0)
    sums = jnp.dot(rows, block_ones, precision=highest, preferred_element_type=jnp.float32)
    quarter_count = (MAP_H * MAP_W // 4) * 32.0
    whole = jnp.sum(sums[:4], axis=0, keepdims=True) * (0.25 / quarter_count)
    return [jnp.where(single, whole, sums[i : i + 1] * (1.0 / quarter_count)) for i in range(4)]


def normalise(parts, single, block_ones):
    means = region_mean(parts, single, block_ones)
    centred = [part - mean[None] for part, mean in zip(parts, means)]
    spread = region_mean([part * part for part in centred], single, block_ones)
    rates = [lax.rsqrt(value + epsilon) for value in spread]
    return [part * rate[None] for part, rate in zip(centred, rates)], rates


def group_ones():
    row = lax.broadcasted_iota(jnp.int32, (CHUNK, CHUNK), 0) // 32
    col = lax.broadcasted_iota(jnp.int32, (CHUNK, CHUNK), 1) // 32
    return (row == col).astype(jnp.float32)


def put_shifts(values, single, taps, lanes):
    pixel = lax.broadcasted_iota(jnp.int32, values.shape, 0) % MAP_W
    for s in range(3):
        if s == 1:
            moved = values
        elif s == 2:
            moved = pltpu.roll(values, MAP_H * MAP_W - 1, 0)
            moved = jnp.where(
                (pixel != MAP_W - 1) & (single | (pixel != MAP_W // 2 - 1)), moved, 0.0
            )
        else:
            moved = pltpu.roll(values, 1, 0)
            moved = jnp.where((pixel != 0) & (single | (pixel != MAP_W // 2)), moved, 0.0)
        low = moved.astype(jnp.bfloat16)
        blank = jnp.zeros((MAP_W, values.shape[1]), jnp.bfloat16)
        taps[s, 0, 0:32, lanes] = blank
        taps[s, 0, 32:288, lanes] = low[0:256]
        taps[s, 0, 288:320, lanes] = jnp.where(single, moved[256:288], 0.0).astype(jnp.bfloat16)
        taps[s, 1, 0:32, lanes] = jnp.where(single, moved[224:256], 0.0).astype(jnp.bfloat16)
        taps[s, 1, 32:288, lanes] = low[256:512]
        taps[s, 1, 288:320, lanes] = blank


def tap_rows(taps, col_step, row_step, lanes):
    rows = taps[col_step, :, pl.ds(pl.multiple_of(row_step * MAP_W, MAP_W), 256), lanes]
    return rows.reshape(MAP_H * MAP_W, rows.shape[-1])


def own_first(start, core, width):
    return pl.ds(pl.multiple_of((start + core * 512) % 1024, width), width)


def forward_conv_kernel(finish, info, x, scale, shift, w_own, w_far, *refs):
    if finish:
        pixels, ln_gain, low_out, joined_out, normed_out, taps, acc = refs
    else:
        low_out, acc, taps = refs
    t = pl.program_id(0)
    core = info[0]
    single = info[1] == 1

    @pl.when(t == 0)
    def _():
        ones = group_ones()
        for start in range(0, 1024, CHUNK):
            lanes = pl.ds(start, CHUNK)
            parts = quadrants(x[:, lanes].astype(jnp.float32))
            normed, _ = normalise(parts, single, ones)
            pre = rejoin(normed) * scale[:, lanes] + shift[:, lanes]
            act = pre * jax.nn.sigmoid(pre)
            low_out[:, lanes] = act.astype(jnp.bfloat16)
            put_shifts(act, single, taps, own_first(start, core, CHUNK))

    rows = tap_rows(taps, t % 3, t // 3, slice(None))
    fresh = jnp.dot(rows[:, :512], w_own[0], preferred_element_type=jnp.float32)
    fresh += jnp.dot(rows[:, 512:], w_far[0], preferred_element_type=jnp.float32)

    @pl.when(t == 0)
    def _():
        acc[...] = fresh

    @pl.when(t > 0)
    def _():
        acc[...] += fresh

    if finish:

        @pl.when(t == 8)
        def _():
            joined = (pixels[...].astype(jnp.float32) + acc[...]) * inv_root_two
            joined_out[...] = joined
            centre = joined - jnp.mean(joined, axis=1, keepdims=True)
            rate = lax.rsqrt(jnp.mean(centre * centre, axis=1, keepdims=True) + epsilon)
            normed_out[...] = (centre * rate * ln_gain[...]).astype(jnp.bfloat16)


def whole(shape):
    return pl.BlockSpec(shape, lambda t, *_: (0,) * len(shape))


def forward_conv(info, x, scale, shift, w_own, w_far, extra=None):
    finish = extra is not None
    full = jax.ShapeDtypeStruct((512, 1024), jnp.float32)
    low = jax.ShapeDtypeStruct((512, 1024), jnp.bfloat16)
    field = whole((512, 1024))
    row = whole((1, 1024))
    tap = pl.BlockSpec((1, 512, 1024), lambda t, *_: (t, 0, 0))
    scratch = [pltpu.VMEM((3, 2, HALF_ROWS, 1024), jnp.bfloat16)]
    if finish:
        scratch += [pltpu.VMEM((512, 1024), jnp.float32)]
    return pl.pallas_call(
        functools.partial(forward_conv_kernel, finish),
        out_shape=(low, full, low) if finish else (low, full),
        grid_spec=pltpu.PrefetchScalarGridSpec(
            num_scalar_prefetch=1,
            grid=(9,),
            in_specs=[field, row, row, tap, tap] + ([field, row] if finish else []),
            out_specs=(field, field, field) if finish else (field, field),
            scratch_shapes=scratch,
        ),
        compiler_params=pltpu.CompilerParams(vmem_limit_bytes=56 << 20),
        name="forward_conv",
    )(info, x, scale, shift, w_own, w_far, *(extra or ()))


def backward_conv_kernel(add, info, weight, grad, x, scale, shift, w_own, w_far, *refs):
    if add:
        passed, result, sums_out, taps, acc = refs
    else:
        result, weighted, sums_out, taps, acc = refs
    t = pl.program_id(0)
    core = info[0]
    single = info[1] == 1

    @pl.when(t == 0)
    def _():
        for start in range(0, 1024, CHUNK):
            lanes = pl.ds(start, CHUNK)
            put_shifts(grad[:, lanes].astype(jnp.float32), single, taps, lanes)

    rows = tap_rows(taps, 2 - t % 3, 2 - t // 3, slice(None))
    last = (((1,), (1,)), ((), ()))
    fresh_own = lax.dot_general(rows, w_own[0], last, preferred_element_type=jnp.float32)
    fresh_far = lax.dot_general(rows, w_far[0], last, preferred_element_type=jnp.float32)

    @pl.when(t == 0)
    def _():
        acc[:, :512] = fresh_own
        acc[:, 512:] = fresh_far

    @pl.when(t > 0)
    def _():
        acc[:, :512] += fresh_own
        acc[:, 512:] += fresh_far

    @pl.when(t == 8)
    def _():
        ones = group_ones()
        for start in range(0, 1024, CHUNK):
            lanes = pl.ds(start, CHUNK)
            parts = quadrants(x[:, lanes].astype(jnp.float32))
            normed, rates = normalise(parts, single, ones)
            gains = scale[:, lanes]
            pre = [part * gains[None] + shift[:, lanes][None] for part in normed]
            grads = quadrants(acc[:, own_first(start, core, CHUNK)])
            sig = [jax.nn.sigmoid(part) for part in pre]
            grads = [g * s * (1.0 + v * (1.0 - s)) for g, s, v in zip(grads, sig, pre)]
            gain_sum = sum(
                jnp.sum(g * n, axis=(0, 1), keepdims=True).reshape(1, CHUNK)
                for g, n in zip(grads, normed)
            )
            bias_sum = sum(
                jnp.sum(g, axis=(0, 1), keepdims=True).reshape(1, CHUNK) for g in grads
            )
            sums_out[0:1, lanes] = gain_sum
            sums_out[1:2, lanes] = bias_sum
            grads = [g * gains[None] for g in grads]
            mean = region_mean(grads, single, ones)
            slope = region_mean([g * n for g, n in zip(grads, normed)], single, ones)
            back = rejoin(
                [
                    r[None] * (g - m[None] - n * s[None])
                    for r, g, m, n, s in zip(rates, grads, mean, normed, slope)
                ]
            )
            if add:
                back += passed[:, lanes] * inv_root_two
                result[:, lanes] = back.astype(jnp.bfloat16)
            else:
                result[:, lanes] = back.astype(jnp.bfloat16)
                weighted[:, lanes] = (back * weight[0]).astype(jnp.bfloat16)


def backward_conv(info, weight, grad, x, scale, shift, w_own, w_far, passed=None):
    add = passed is not None
    low = jax.ShapeDtypeStruct((512, 1024), jnp.bfloat16)
    sums = jax.ShapeDtypeStruct((2, 1024), jnp.float32)
    field = whole((512, 1024))
    row = whole((1, 1024))
    pair = whole((2, 1024))
    tap = pl.BlockSpec((1, 512, 1024), lambda t, *_: (t, 0, 0))
    return pl.pallas_call(
        functools.partial(backward_conv_kernel, add),
        out_shape=(low, sums) if add else (low, low, sums),
        grid_spec=pltpu.PrefetchScalarGridSpec(
            num_scalar_prefetch=2,
            grid=(9,),
            in_specs=[field, field, row, row, tap, tap] + ([field] if add else []),
            out_specs=(field, pair) if add else (field, field, pair),
            scratch_shapes=[
                pltpu.VMEM((3, 2, HALF_ROWS, 1024), jnp.bfloat16),
                pltpu.VMEM((512, 1024), jnp.float32),
            ],
        ),
        compiler_params=pltpu.CompilerParams(vmem_limit_bytes=56 << 20),
        name="backward_conv",
    )(info, weight, grad, x, scale, shift, w_own, w_far, *([passed] if add else []))


def conv_term_kernel(layouts, a0, a1, a2, a3, b_own, b_far, out, taps):
    t = pl.program_id(0)

    @pl.when(t == 0)
    def _():
        for j in range(4):
            for e, b in enumerate((b_own, b_far)):
                put_shifts(
                    b[j].astype(jnp.float32), layouts[2 * j + e] == 1, taps.at[2 * j + e], slice(None)
                )

    total = jnp.zeros((512, CHUNK), jnp.float32)
    for j, a in enumerate((a0, a1, a2, a3)):
        for e in range(2):
            rows = tap_rows(taps.at[2 * j + e], 2 - t % 3, 2 - t // 3, slice(None))
            total += jnp.dot(a[e], rows, preferred_element_type=jnp.float32)
    out[0] = total.astype(jnp.bfloat16)


def conv_term(layouts, sources, b_own, b_far):
    return pl.pallas_call(
        conv_term_kernel,
        out_shape=jax.ShapeDtypeStruct((9, 512, CHUNK), jnp.bfloat16),
        grid_spec=pltpu.PrefetchScalarGridSpec(
            num_scalar_prefetch=1,
            grid=(9,),
            in_specs=[whole((2, 512, 512))] * 4 + [whole((4, 512, CHUNK))] * 2,
            out_specs=pl.BlockSpec((1, 512, CHUNK), lambda t, *_: (t, 0, 0)),
            scratch_shapes=[pltpu.VMEM((8, 3, 2, HALF_ROWS, CHUNK), jnp.bfloat16)],
        ),
        compiler_params=pltpu.CompilerParams(vmem_limit_bytes=56 << 20),
        name="conv_term",
    )(layouts, *sources, b_own, b_far)


def text_term_kernel(a0, a1, a2, a3, b_own, b_far, out):
    left = jnp.concatenate([a[e] for a in (a0, a1, a2, a3) for e in range(2)], axis=1)
    right = jnp.concatenate([b[j] for j in range(4) for b in (b_own, b_far)], axis=0)
    total = jnp.dot(left, right, preferred_element_type=jnp.float32).astype(jnp.bfloat16)
    out[0] = total[:, :CHUNK]
    out[1] = total[:, CHUNK:]


def text_term(sources, b_own, b_far):
    rows = pl.BlockSpec((2, 512, TEXT_LEN), lambda i: (0, i, 0))
    cols = pl.BlockSpec((4, TEXT_LEN, 2 * CHUNK), lambda i: (0, 0, 0))
    return pl.pallas_call(
        text_term_kernel,
        out_shape=jax.ShapeDtypeStruct((8, 512, CHUNK), jnp.bfloat16),
        grid=(4,),
        in_specs=[rows] * 4 + [cols] * 2,
        out_specs=pl.BlockSpec((2, 512, CHUNK), lambda i: (i, 0, 0)),
        name="text_term",
    )(*sources, b_own, b_far)


def attn_term_kernel(normed_own, normed_far, mixed_own, mixed_far, t_own, t_far, c_own, c_far, out):
    j = pl.program_id(1)

    @pl.when(j < 3)
    def _():
        total = jnp.dot(normed_own[...], t_own[...], preferred_element_type=jnp.float32)
        total += jnp.dot(normed_far[...], t_far[...], preferred_element_type=jnp.float32)
        out[0, 0] = total.astype(jnp.bfloat16)

    @pl.when(j == 3)
    def _():
        total = jnp.dot(mixed_own[...], c_own[...], preferred_element_type=jnp.float32)
        total += jnp.dot(mixed_far[...], c_far[...], preferred_element_type=jnp.float32)
        out[0, 0] = total.astype(jnp.bfloat16)


def attn_term(normed_pair, mixed_pair, triple_pair, cot_pair):
    left = pl.BlockSpec((512, 512), lambda q, j: (0, 0))
    triple = pl.BlockSpec((512, CHUNK), lambda q, j: (0, 4 * jnp.minimum(j, 2) + q))
    cot = pl.BlockSpec((512, CHUNK), lambda q, j: (0, q))
    return pl.pallas_call(
        attn_term_kernel,
        out_shape=jax.ShapeDtypeStruct((4, 4, 512, CHUNK), jnp.bfloat16),
        grid=(4, 4),
        in_specs=[left] * 4 + [triple] * 2 + [cot] * 2,
        out_specs=pl.BlockSpec((1, 1, 512, CHUNK), lambda q, j: (q, j, 0, 0)),
        name="attn_term",
    )(*normed_pair, *mixed_pair, *triple_pair, *cot_pair)


def to_wide(value, step):
    return lax.ppermute(value, "wide", [(i, i ^ step) for i in range(16)])


def to_far(value):
    return lax.ppermute(value, "narrow", [(0, 1), (1, 0)])


def gather_all(row):
    rows = row[None]
    rows = jnp.concatenate([rows, to_far(rows)])
    for step in (1, 2, 4, 8):
        rows = jnp.concatenate([rows, to_wide(rows, step)])
    return rows


def half_of(value, core, axis):
    size = value.shape[axis] // 2
    return lax.dynamic_slice_in_dim(value, core * size, size, axis)


def share_source(value_t, core):
    far = to_far(half_of(value_t, 1 - core, 0))
    pair = jnp.stack([half_of(value_t, core, 0), far])
    return (pair, to_wide(pair, 1), to_wide(pair, 2), to_wide(pair, 3))


def share_grad(grad, place):
    rows, blocks, _ = grad.shape
    found = []
    for step in range(4):
        start = CHUNK * jnp.bitwise_xor(place, step)
        piece = lax.dynamic_slice_in_dim(grad, start, CHUNK, 2).reshape(rows, blocks * CHUNK)
        found.append(to_wide(piece, step) if step else piece)
    own = jnp.stack(found)
    return own, to_far(own)


def pair_body(
    pixels,
    layout,
    noise_group,
    cond_embed,
    text_embed,
    cotangent,
    gn_gain,
    gn_bias,
    conv_in,
    film_weight,
    film_bias,
    conv_out,
    ln_gain,
    qkv_weight,
    out_weight,
    text_weight,
):
    f32, bf16 = jnp.float32, jnp.bfloat16
    wide = lax.axis_index("wide")
    core = lax.axis_index("narrow")
    place = wide % 4
    group_total = lax.axis_size("wide")

    conv_in_far = to_far(conv_in)
    vectors = jnp.concatenate([gn_gain, gn_bias, ln_gain, film_bias])
    vectors_far = to_far(vectors)
    low_vec = jnp.where(core == 0, vectors, vectors_far)
    high_vec = jnp.where(core == 0, vectors_far, vectors)

    def joined_vec(start, size):
        return jnp.concatenate([low_vec[start : start + size], high_vec[start : start + size]])

    gain_row = joined_vec(0, 512).astype(f32)[None]
    bias_row = joined_vec(512, 512).astype(f32)[None]
    ln_row = joined_vec(1024, 512).astype(f32)[None]
    film_bias_full = joined_vec(1536, 1024).astype(f32)
    conv_out_far = to_far(conv_out)

    facts = jnp.stack([noise_group[0], layout[0]])
    facts = jnp.pad(facts.astype(f32), (0, 126))
    early = gather_all(jnp.concatenate([cond_embed[0].astype(f32), facts]))
    cond_all = early[:, :1024]
    alike = jnp.sum((early[:, 1024] == facts[0]).astype(f32))
    weight = 1.0 / (group_total * alike)
    info = jnp.stack([core.astype(jnp.int32), layout[0]])
    layouts = early[:8, 1025].astype(jnp.int32)
    weight_row = weight.reshape(1)

    text_one = text_embed[0]
    text_sources = share_source(text_one.T, core)
    cot = cotangent[0]
    film_full = lax.all_gather(film_weight, "narrow", axis=0, tiled=True)
    qkv_full = lax.all_gather(qkv_weight, "narrow", axis=0, tiled=True)
    out_full = lax.all_gather(out_weight, "narrow", axis=0, tiled=True)
    text_full = lax.all_gather(text_weight, "narrow", axis=0, tiled=True)

    region_ids = region_ids_of(layout[0])
    field = pixels[0]
    condition = jax.nn.silu(cond_embed[0].astype(f32)).astype(bf16)
    film_out = jnp.dot(condition, film_full, preferred_element_type=f32) + film_bias_full
    film_scale = 1.0 + film_out[None, :1024]
    film_shift = film_out[None, 1024:]

    first_low, hidden_one = forward_conv(info, field, gain_row, bias_row, conv_in, conv_in_far)
    first_sources = share_source(first_low.T, core)
    second_low, joined, normed = forward_conv(
        info, hidden_one, film_scale, film_shift, conv_out, conv_out_far, (field, ln_row)
    )
    second_sources = share_source(second_low.T, core)

    attn_full = (ln_row[0], qkv_full, out_full, text_full)
    result, stored = attention_mid(normed, joined, text_one, region_ids, attn_full)
    output = result.astype(bf16)
    grad_joined, ln_term, grad_triple, grad_pair = attention_back(
        cot, joined, stored, attn_full
    )
    mixed = stored[5]
    grad_two = grad_joined * inv_root_two
    grad_two_low = grad_two.astype(bf16)

    triple_w = (weight * grad_triple).astype(bf16)
    pair_w = (weight * grad_pair).astype(bf16)
    cot_w = (weight * cot.astype(f32)).astype(bf16)
    two_w = (weight * grad_two).astype(bf16)

    pair_own, pair_far = share_grad(pair_w.reshape(TEXT_LEN, 2, 1024), place)
    text_part = text_term(text_sources, pair_own, pair_far)

    normed_t, mixed_t = normed.T, mixed.T
    normed_pair = (half_of(normed_t, core, 0), to_far(half_of(normed_t, 1 - core, 0)))
    mixed_pair = (half_of(mixed_t, core, 0), to_far(half_of(mixed_t, 1 - core, 0)))
    attn_part = attn_term(
        normed_pair, mixed_pair, (triple_w, to_far(triple_w)), (cot_w, to_far(cot_w))
    )
    plane = [[4 * z + i for i in range(4)] for z in range(4)]
    attn_part = lax.psum_scatter(
        attn_part, "wide", scatter_dimension=0, axis_index_groups=plane, tiled=True
    )[0]

    two_own, two_far = share_grad(two_w.reshape(512, 1, 1024), place)
    conv_out_part = conv_term(layouts, second_sources, two_own, two_far)

    hidden_low, hidden_w, film_sums = backward_conv(
        info, weight_row, grad_two_low, hidden_one, film_scale, film_shift, conv_out, conv_out_far
    )
    hid_own, hid_far = share_grad(hidden_w.reshape(512, 1, 1024), place)
    conv_in_part = conv_term(layouts, first_sources, hid_own, hid_far)
    input_grad, gn_sums = backward_conv(
        info, weight_row, hidden_low, field, gain_row, bias_row, conv_in, conv_in_far, grad_joined
    )

    small = jnp.concatenate(
        [film_sums.reshape(-1), gn_sums.reshape(-1), ln_term.reshape(-1)]
    )
    small_all = gather_all(weight * small)
    cond_low = jax.nn.silu(cond_all).astype(bf16)
    grad_film_weight = lax.dot_general(
        half_of(cond_low, core, 1),
        small_all[:, :2048].astype(bf16),
        (((0,), (0,)), ((), ())),
        preferred_element_type=f32,
    )
    small_sum = jnp.sum(small_all, axis=0)
    grad_film_bias = half_of(small_sum[:2048], core, 0)
    grad_gn_gain = half_of(small_sum[2048:3072], core, 0)
    grad_gn_bias = half_of(small_sum[3072:4096], core, 0)
    grad_ln_gain = half_of(small_sum[4096:], core, 0)

    grad_text, grad_qkv, grad_out, grad_conv_out, grad_conv_in = sum_and_gather(
        text_part, attn_part, conv_out_part, conv_in_part
    )
    return (
        output[None],
        input_grad[None],
        grad_gn_gain,
        grad_gn_bias,
        grad_conv_in.astype(f32),
        grad_film_weight,
        grad_film_bias,
        grad_conv_out.astype(f32),
        grad_ln_gain,
        grad_qkv.astype(f32),
        grad_out.astype(f32),
        grad_text.astype(f32),
    )


def attention_mid(normed_low, joined, text_one, region_ids, attn_full):
    _, qkv_full, out_full, text_full = attn_full
    pixel_count, channels = joined.shape
    head_dim = channels // HEADS
    score_scale = head_dim ** (-0.5)
    triple = jnp.dot(normed_low, qkv_full, preferred_element_type=jnp.float32).astype(jnp.bfloat16)
    text_pair = jnp.dot(text_one, text_full, preferred_element_type=jnp.float32).astype(
        jnp.bfloat16
    )
    queries = triple[:, :channels].reshape(pixel_count, HEADS, head_dim)
    key_rows = jnp.concatenate(
        [triple[:, channels : 2 * channels], text_pair[:, :channels]], axis=0
    ).reshape(-1, HEADS, head_dim)
    value_rows = jnp.concatenate(
        [triple[:, 2 * channels :], text_pair[:, channels:]], axis=0
    ).reshape(-1, HEADS, head_dim)
    allowed = allowed_keys(region_ids)
    masked = jnp.where(
        allowed[None],
        jnp.einsum("phd,jhd->hpj", queries, key_rows, preferred_element_type=jnp.float32)
        * score_scale,
        masked_score,
    )
    row_peak = jnp.max(masked, axis=2, keepdims=True)
    exponent = jnp.exp(masked - row_peak)
    exp_total = jnp.sum(exponent, axis=2, keepdims=True)
    attn_probs = exponent / exp_total
    log_total = row_peak + jnp.log(exp_total)
    mixed = (
        jnp.einsum(
            "hpj,jhd->phd",
            attn_probs.astype(jnp.bfloat16),
            value_rows,
            preferred_element_type=jnp.float32,
        )
        .reshape(pixel_count, channels)
        .astype(jnp.bfloat16)
    )
    result = joined + jnp.dot(mixed, out_full, preferred_element_type=jnp.float32)
    return (result, (normed_low, queries, key_rows, value_rows, log_total, mixed, allowed))


def attention_back(grad_result, joined, stored, attn_full):
    gain_row, qkv_full, out_full, text_full = attn_full
    normed_low, queries, key_rows, value_rows, log_total, mixed, allowed = stored
    pixel_count, channels = joined.shape
    head_dim = channels // HEADS
    score_scale = head_dim ** (-0.5)
    grad_mixed = (
        jnp.einsum("pd,cd->pc", grad_result, out_full, preferred_element_type=jnp.float32)
        .astype(jnp.bfloat16)
        .reshape(pixel_count, HEADS, head_dim)
    )
    masked = jnp.where(
        allowed[None],
        jnp.einsum("phd,jhd->hpj", queries, key_rows, preferred_element_type=jnp.float32)
        * score_scale,
        masked_score,
    )
    attn_probs = jnp.exp(masked - log_total)
    grad_probs = jnp.einsum(
        "phd,jhd->hpj", grad_mixed, value_rows, preferred_element_type=jnp.float32
    )
    grad_values = jnp.einsum(
        "hpj,phd->jhd",
        attn_probs.astype(jnp.bfloat16),
        grad_mixed,
        preferred_element_type=jnp.float32,
    )
    row_inner = jnp.sum(attn_probs * grad_probs, axis=2, keepdims=True)
    grad_scores = (attn_probs * (grad_probs - row_inner)).astype(jnp.bfloat16)
    grad_queries = (
        jnp.einsum("hpj,jhd->phd", grad_scores, key_rows, preferred_element_type=jnp.float32)
        * score_scale
    )
    grad_keys = (
        jnp.einsum("hpj,phd->jhd", grad_scores, queries, preferred_element_type=jnp.float32)
        * score_scale
    )
    grad_triple = jnp.concatenate(
        [
            grad_queries.reshape(pixel_count, channels),
            grad_keys[:pixel_count].reshape(pixel_count, channels),
            grad_values[:pixel_count].reshape(pixel_count, channels),
        ],
        axis=1,
    )
    grad_pair = jnp.concatenate(
        [
            grad_keys[pixel_count:].reshape(-1, channels),
            grad_values[pixel_count:].reshape(-1, channels),
        ],
        axis=1,
    )
    grad_normed = jnp.einsum(
        "pk,ck->pc", grad_triple.astype(jnp.bfloat16), qkv_full, preferred_element_type=jnp.float32
    )
    _, norm_back = jax.vjp(layer_norm, joined, gain_row)
    grad_joined_norm, term_gain = norm_back(grad_normed)
    return (grad_result.astype(jnp.float32) + grad_joined_norm, term_gain, grad_triple, grad_pair)


def solution(mesh):
    fits = mesh.shape["wide"] == 16 and mesh.shape["narrow"] == 2
    body = pair_body if fits else plain_body
    placed = (
        P(("wide", "narrow"), None, None),
        P(("wide", "narrow")),
        P(("wide", "narrow")),
        P(("wide", "narrow"), None),
        P(("wide", "narrow"), None, None),
        P(("wide", "narrow"), None, None),
        P("narrow"),
        P("narrow"),
        P(None, "narrow", None),
        P("narrow", None),
        P("narrow"),
        P(None, "narrow", None),
        P("narrow"),
        P("narrow", None),
        P("narrow", None),
        P("narrow", None),
    )
    return jax.shard_map(
        body,
        mesh=mesh,
        in_specs=placed,
        out_specs=(
            P(("wide", "narrow"), None, None),
            P(("wide", "narrow"), None, None),
            P("narrow"),
            P("narrow"),
            P(None, "narrow", None),
            P("narrow", None),
            P("narrow"),
            P(None, "narrow", None),
            P("narrow"),
            P("narrow", None),
            P("narrow", None),
            P("narrow", None),
        ),
        check_vma=False,
    )
```

```python
import functools

import jax
import jax.numpy as jnp
from jax import lax
from jax.experimental import pallas as pl
from jax.experimental.pallas import tpu as pltpu
from jax.sharding import PartitionSpec as P

NORM_GROUPS = 32
HEADS = 8
TEXT_LEN = 128
MAP_H = 16
MAP_W = 32


highest = lax.Precision.HIGHEST
epsilon = 1e-05
inv_root_two = 0.7071067811865476
masked_score = -1e30


def region_ids_of(layout_value):
    position = jnp.arange(MAP_H * MAP_W, dtype=jnp.int32)
    quarter = 2 * (position // MAP_W >= MAP_H // 2).astype(jnp.int32) + (
        position % MAP_W >= MAP_W // 2
    ).astype(jnp.int32)
    return jnp.where(layout_value == 1, jnp.zeros_like(quarter), quarter)


def tap_validity(region_ids):
    code_grid = region_ids.reshape(MAP_H, MAP_W)
    padded = jnp.pad(code_grid, 1, constant_values=-1)
    found = []
    for row_step in (-1, 0, 1):
        for col_step in (-1, 0, 1):
            neighbour = padded[
                1 + row_step : 1 + row_step + MAP_H, 1 + col_step : 1 + col_step + MAP_W
            ]
            found.append((neighbour == code_grid).reshape(-1))
    return jnp.stack(found)


def unfold(values, tap_valid):
    channels = values.shape[-1]
    padded = jnp.pad(values.reshape(MAP_H, MAP_W, channels), ((1, 1), (1, 1), (0, 0)))
    pieces = []
    tap_index = 0
    for row_step in (-1, 0, 1):
        for col_step in (-1, 0, 1):
            neighbour = padded[
                1 + row_step : 1 + row_step + MAP_H, 1 + col_step : 1 + col_step + MAP_W
            ].reshape(MAP_H * MAP_W, channels)
            pieces.append(
                jnp.where(tap_valid[tap_index][:, None], neighbour, jnp.zeros_like(neighbour))
            )
            tap_index += 1
    return jnp.concatenate(pieces, axis=1)


def fold_back(grad_cols, tap_valid):
    channels = grad_cols.shape[1] // 9
    start_point = jnp.zeros((grad_cols.shape[0], channels), jnp.float32)
    unfolded, pullback = jax.vjp(lambda field: unfold(field, tap_valid), start_point)
    return pullback(grad_cols)[0]


def group_norm(values, members):
    pixel_count, channels = values.shape
    grouped = values.reshape(pixel_count, NORM_GROUPS, channels // NORM_GROUPS)
    counts = jnp.maximum(jnp.sum(members, axis=0) * (channels // NORM_GROUPS), 1.0)
    region_sums = jnp.einsum("pr,pg->rg", members, jnp.sum(grouped, axis=2), precision=highest)
    pixel_means = jnp.einsum("pr,rg->pg", members, region_sums / counts[:, None], precision=highest)
    centred = grouped - pixel_means[:, :, None]
    squares = jnp.einsum(
        "pr,pg->rg", members, jnp.sum(centred * centred, axis=2), precision=highest
    )
    spreads = jnp.einsum(
        "pr,rg->pg", members, lax.rsqrt(squares / counts[:, None] + epsilon), precision=highest
    )
    return (centred * spreads[:, :, None]).reshape(pixel_count, channels)


def layer_norm(field, gain_in):
    centre = field - jnp.mean(field, axis=1, keepdims=True)
    return centre * lax.rsqrt(jnp.mean(centre * centre, axis=1, keepdims=True) + epsilon) * gain_in


def first_block(field, gain_in, bias_in, members):
    return jax.nn.silu(group_norm(field, members) * gain_in + bias_in)


def mid_block(hidden_in, film_in, members):
    channels = hidden_in.shape[1]
    return jax.nn.silu(
        group_norm(hidden_in, members) * (1.0 + film_in[:channels]) + film_in[channels:]
    )


def residual_front(field, members, tap_valid, condition, weights_full):
    gain_full, bias_full, conv_first, film_full, film_bias_full, conv_second = weights_full
    channels = field.shape[1]
    first_act, first_back = jax.vjp(
        lambda field_in, gain_in, bias_in: first_block(field_in, gain_in, bias_in, members),
        field,
        gain_full.astype(jnp.float32),
        bias_full.astype(jnp.float32),
    )
    first_low = first_act.astype(jnp.bfloat16)
    first_cols = unfold(first_low, tap_valid)
    hidden_one = jnp.dot(
        first_cols, conv_first.reshape(-1, channels), preferred_element_type=jnp.float32
    )
    film_out = jnp.dot(
        condition, film_full, preferred_element_type=jnp.float32
    ) + film_bias_full.astype(jnp.float32)
    second_act, mid_back = jax.vjp(
        lambda hidden_in, film_in: mid_block(hidden_in, film_in, members), hidden_one, film_out
    )
    second_low = second_act.astype(jnp.bfloat16)
    second_cols = unfold(second_low, tap_valid)
    return (first_cols, second_cols, first_back, mid_back)


def allowed_keys(region_ids):
    same_region = region_ids[:, None] == region_ids[None, :]
    return jnp.concatenate(
        [same_region, jnp.ones((region_ids.shape[0], TEXT_LEN), dtype=jnp.bool_)], axis=1
    )


def attention_forward(joined, text_one, region_ids, attn_full):
    gain_full, qkv_full, out_full, text_full = attn_full
    pixel_count, channels = joined.shape
    head_dim = channels // HEADS
    score_scale = head_dim ** (-0.5)
    normed_low = layer_norm(joined, gain_full.astype(jnp.float32)).astype(jnp.bfloat16)
    triple = jnp.dot(normed_low, qkv_full, preferred_element_type=jnp.float32).astype(jnp.bfloat16)
    text_pair = jnp.dot(text_one, text_full, preferred_element_type=jnp.float32).astype(
        jnp.bfloat16
    )
    queries = triple[:, :channels].reshape(pixel_count, HEADS, head_dim)
    key_rows = jnp.concatenate(
        [triple[:, channels : 2 * channels], text_pair[:, :channels]], axis=0
    ).reshape(-1, HEADS, head_dim)
    value_rows = jnp.concatenate(
        [triple[:, 2 * channels :], text_pair[:, channels:]], axis=0
    ).reshape(-1, HEADS, head_dim)
    allowed = allowed_keys(region_ids)
    masked = jnp.where(
        allowed[None],
        jnp.einsum("phd,jhd->hpj", queries, key_rows, preferred_element_type=jnp.float32)
        * score_scale,
        masked_score,
    )
    row_peak = jnp.max(masked, axis=2, keepdims=True)
    exponent = jnp.exp(masked - row_peak)
    exp_total = jnp.sum(exponent, axis=2, keepdims=True)
    attn_probs = exponent / exp_total
    log_total = row_peak + jnp.log(exp_total)
    mixed = (
        jnp.einsum(
            "hpj,jhd->phd",
            attn_probs.astype(jnp.bfloat16),
            value_rows,
            preferred_element_type=jnp.float32,
        )
        .reshape(pixel_count, channels)
        .astype(jnp.bfloat16)
    )
    result = joined + jnp.dot(mixed, out_full, preferred_element_type=jnp.float32)
    return (result, (normed_low, queries, key_rows, value_rows, log_total, mixed, allowed))


def attention_backward(grad_result, joined, text_one, stored, attn_full):
    gain_full, qkv_full, out_full, text_full = attn_full
    normed_low, queries, key_rows, value_rows, log_total, mixed, allowed = stored
    pixel_count, channels = joined.shape
    head_dim = channels // HEADS
    score_scale = head_dim ** (-0.5)
    grad_mixed = (
        jnp.einsum("pd,cd->pc", grad_result, out_full, preferred_element_type=jnp.float32)
        .astype(jnp.bfloat16)
        .reshape(pixel_count, HEADS, head_dim)
    )
    masked = jnp.where(
        allowed[None],
        jnp.einsum("phd,jhd->hpj", queries, key_rows, preferred_element_type=jnp.float32)
        * score_scale,
        masked_score,
    )
    attn_probs = jnp.exp(masked - log_total)
    grad_probs = jnp.einsum(
        "phd,jhd->hpj", grad_mixed, value_rows, preferred_element_type=jnp.float32
    )
    grad_values = jnp.einsum(
        "hpj,phd->jhd",
        attn_probs.astype(jnp.bfloat16),
        grad_mixed,
        preferred_element_type=jnp.float32,
    )
    row_inner = jnp.sum(attn_probs * grad_probs, axis=2, keepdims=True)
    grad_scores = (attn_probs * (grad_probs - row_inner)).astype(jnp.bfloat16)
    grad_queries = (
        jnp.einsum("hpj,jhd->phd", grad_scores, key_rows, preferred_element_type=jnp.float32)
        * score_scale
    )
    grad_keys = (
        jnp.einsum("hpj,phd->jhd", grad_scores, queries, preferred_element_type=jnp.float32)
        * score_scale
    )
    grad_triple = jnp.concatenate(
        [
            grad_queries.reshape(pixel_count, channels),
            grad_keys[:pixel_count].reshape(pixel_count, channels),
            grad_values[:pixel_count].reshape(pixel_count, channels),
        ],
        axis=1,
    ).astype(jnp.bfloat16)
    grad_pair = jnp.concatenate(
        [
            grad_keys[pixel_count:].reshape(-1, channels),
            grad_values[pixel_count:].reshape(-1, channels),
        ],
        axis=1,
    ).astype(jnp.bfloat16)
    term_out = jnp.einsum("pc,pd->cd", mixed, grad_result, preferred_element_type=jnp.float32)
    term_qkv = jnp.einsum("pc,pk->ck", normed_low, grad_triple, preferred_element_type=jnp.float32)
    term_text = jnp.einsum("tc,tk->ck", text_one, grad_pair, preferred_element_type=jnp.float32)
    big_terms = (term_qkv, term_out, term_text)
    grad_normed = jnp.einsum("pk,ck->pc", grad_triple, qkv_full, preferred_element_type=jnp.float32)
    normed_value, norm_back = jax.vjp(layer_norm, joined, gain_full.astype(jnp.float32))
    grad_joined_norm, term_gain = norm_back(grad_normed)
    return (grad_result.astype(jnp.float32) + grad_joined_norm, term_gain, big_terms)


def every_wide_sum(parts):
    return (
        lax.psum(parts[0].astype(jnp.bfloat16), "wide").astype(jnp.float32),
        lax.psum(parts[1].astype(jnp.bfloat16), "wide").astype(jnp.float32),
        lax.psum(parts[2].astype(jnp.bfloat16), "wide").astype(jnp.float32),
        lax.psum(parts[3].astype(jnp.bfloat16), "wide").astype(jnp.float32),
        lax.psum(parts[4].astype(jnp.bfloat16), "wide").astype(jnp.float32),
        lax.psum(parts[5].astype(jnp.bfloat16), "wide").astype(jnp.float32),
        lax.psum(parts[6].astype(jnp.bfloat16), "wide").astype(jnp.float32),
        lax.psum(parts[7].astype(jnp.bfloat16), "wide").astype(jnp.float32),
        lax.psum(parts[8].astype(jnp.bfloat16), "wide").astype(jnp.float32),
        lax.psum(parts[9].astype(jnp.bfloat16), "wide").astype(jnp.float32),
    )


def plain_body(
    pixels,
    layout,
    noise_group,
    cond_embed,
    text_embed,
    cotangent,
    gn_gain,
    gn_bias,
    conv_in,
    film_weight,
    film_bias,
    conv_out,
    ln_gain,
    qkv_weight,
    out_weight,
    text_weight,
):
    group_total = lax.axis_size("wide")
    onehot_groups = (
        noise_group[:, None] == jnp.arange(group_total, dtype=jnp.int32)[None, :]
    ).astype(jnp.float32)
    counts = lax.psum(jnp.sum(onehot_groups, axis=0), ("wide", "narrow"))
    slot_weights = 1.0 / (group_total * jnp.sum(onehot_groups * counts[None, :], axis=1))
    res_full = (
        lax.all_gather(gn_gain, "narrow", axis=0, tiled=True),
        lax.all_gather(gn_bias, "narrow", axis=0, tiled=True),
        lax.all_gather(conv_in, "narrow", axis=1, tiled=True),
        lax.all_gather(film_weight, "narrow", axis=0, tiled=True),
        lax.all_gather(film_bias, "narrow", axis=0, tiled=True),
        lax.all_gather(conv_out, "narrow", axis=1, tiled=True),
    )
    attn_full = (
        lax.all_gather(ln_gain, "narrow", axis=0, tiled=True),
        lax.all_gather(qkv_weight, "narrow", axis=0, tiled=True),
        lax.all_gather(out_weight, "narrow", axis=0, tiled=True),
        lax.all_gather(text_weight, "narrow", axis=0, tiled=True),
    )
    channels = pixels.shape[2]
    slot_index = 0
    field = pixels[slot_index].astype(jnp.float32)
    region_ids = region_ids_of(layout[slot_index])
    members = (region_ids[:, None] == jnp.arange(4, dtype=jnp.int32)[None, :]).astype(jnp.float32)
    tap_valid = tap_validity(region_ids)
    condition = jax.nn.silu(cond_embed[slot_index].astype(jnp.float32)).astype(jnp.bfloat16)
    front = residual_front(field, members, tap_valid, condition, res_full)
    hidden_two = jnp.dot(
        front[1], res_full[5].reshape(-1, channels), preferred_element_type=jnp.float32
    )
    joined = (field + hidden_two) * inv_root_two
    result, stored = attention_forward(joined, text_embed[slot_index], region_ids, attn_full)
    outputs = [result.astype(jnp.bfloat16)]
    saved = [(field, members, tap_valid, condition, joined, stored)]
    attn_big = tuple((jnp.zeros(full_weight.shape, jnp.float32) for full_weight in attn_full[1:]))
    slot_index = 0
    field, members, tap_valid, condition, joined, stored = saved[slot_index]
    grad_joined, term_gain, big_terms = attention_backward(
        cotangent[slot_index], joined, text_embed[slot_index], stored, attn_full
    )
    joined_grads = [grad_joined]
    gain_sum = slot_weights[slot_index] * term_gain
    attn_big = tuple((slot_weights[slot_index] * fresh for fresh in big_terms))
    grad_ln_gain, grad_qkv_weight, grad_out_weight, grad_text_weight = (
        lax.psum_scatter(
            gain_sum.astype(jnp.bfloat16), "narrow", scatter_dimension=0, tiled=True
        ).astype(jnp.float32),
        lax.psum_scatter(
            attn_big[0].astype(jnp.bfloat16), "narrow", scatter_dimension=0, tiled=True
        ).astype(jnp.float32),
        lax.psum_scatter(
            attn_big[1].astype(jnp.bfloat16), "narrow", scatter_dimension=0, tiled=True
        ).astype(jnp.float32),
        lax.psum_scatter(
            attn_big[2].astype(jnp.bfloat16), "narrow", scatter_dimension=0, tiled=True
        ).astype(jnp.float32),
    )
    res_back = (
        lax.all_gather(gn_gain, "narrow", axis=0, tiled=True),
        lax.all_gather(gn_bias, "narrow", axis=0, tiled=True),
        lax.all_gather(conv_in, "narrow", axis=1, tiled=True),
        lax.all_gather(film_weight, "narrow", axis=0, tiled=True),
        lax.all_gather(film_bias, "narrow", axis=0, tiled=True),
        lax.all_gather(conv_out, "narrow", axis=1, tiled=True),
    )
    conv_first = res_back[2].reshape(-1, channels)
    conv_second = res_back[5].reshape(-1, channels)
    small_sums = (
        jnp.zeros(res_back[0].shape, jnp.float32),
        jnp.zeros(res_back[1].shape, jnp.float32),
        jnp.zeros(res_back[4].shape, jnp.float32),
    )
    res_big = (
        jnp.zeros(res_back[2].shape, jnp.float32),
        jnp.zeros(res_back[3].shape, jnp.float32),
        jnp.zeros(res_back[5].shape, jnp.float32),
    )
    slot_index = 0
    field, members, tap_valid, condition, joined, stored = saved[slot_index]
    grad_joined = joined_grads[slot_index]
    first_cols, second_cols, first_back, mid_back = residual_front(
        field, members, tap_valid, condition, res_back
    )
    grad_two = (grad_joined * inv_root_two).astype(jnp.bfloat16)
    grad_second = fold_back(
        jnp.einsum("pc,kc->pk", grad_two, conv_second, preferred_element_type=jnp.float32),
        tap_valid,
    )
    grad_hidden, grad_film = mid_back(grad_second)
    grad_film_low = grad_film.astype(jnp.bfloat16)
    grad_one = grad_hidden.astype(jnp.bfloat16)
    grad_first = fold_back(
        jnp.einsum("pc,kc->pk", grad_one, conv_first, preferred_element_type=jnp.float32), tap_valid
    )
    grad_field, term_gain, term_bias = first_back(grad_first)
    input_grads = [(grad_joined * inv_root_two + grad_field).astype(jnp.bfloat16)]
    small_terms = (term_gain, term_bias, grad_film_low.astype(jnp.float32))
    small_sums = tuple((slot_weights[slot_index] * fresh for fresh in small_terms))
    term_conv_out = jnp.einsum(
        "pk,pc->kc", second_cols, grad_two, preferred_element_type=jnp.float32
    )
    term_film = jnp.einsum("k,c->kc", condition, grad_film_low, preferred_element_type=jnp.float32)
    term_conv_in = jnp.einsum("pk,pc->kc", first_cols, grad_one, preferred_element_type=jnp.float32)
    big_terms = (
        term_conv_in.reshape(res_back[2].shape),
        term_film,
        term_conv_out.reshape(res_back[5].shape),
    )
    res_big = tuple((slot_weights[slot_index] * fresh for fresh in big_terms))
    grad_gn_gain, grad_gn_bias, grad_conv_in, grad_film_weight, grad_film_bias, grad_conv_out = (
        lax.psum_scatter(
            small_sums[0].astype(jnp.bfloat16), "narrow", scatter_dimension=0, tiled=True
        ).astype(jnp.float32),
        lax.psum_scatter(
            small_sums[1].astype(jnp.bfloat16), "narrow", scatter_dimension=0, tiled=True
        ).astype(jnp.float32),
        lax.psum_scatter(
            res_big[0].astype(jnp.bfloat16), "narrow", scatter_dimension=1, tiled=True
        ).astype(jnp.float32),
        lax.psum_scatter(
            res_big[1].astype(jnp.bfloat16), "narrow", scatter_dimension=0, tiled=True
        ).astype(jnp.float32),
        lax.psum_scatter(
            small_sums[2].astype(jnp.bfloat16), "narrow", scatter_dimension=0, tiled=True
        ).astype(jnp.float32),
        lax.psum_scatter(
            res_big[2].astype(jnp.bfloat16), "narrow", scatter_dimension=1, tiled=True
        ).astype(jnp.float32),
    )
    (
        grad_gn_gain,
        grad_gn_bias,
        grad_conv_in,
        grad_film_weight,
        grad_film_bias,
        grad_conv_out,
        grad_ln_gain,
        grad_qkv_weight,
        grad_out_weight,
        grad_text_weight,
    ) = every_wide_sum(
        (
            grad_gn_gain,
            grad_gn_bias,
            grad_conv_in,
            grad_film_weight,
            grad_film_bias,
            grad_conv_out,
            grad_ln_gain,
            grad_qkv_weight,
            grad_out_weight,
            grad_text_weight,
        )
    )
    return (
        jnp.stack(outputs),
        jnp.stack(input_grads),
        grad_gn_gain,
        grad_gn_bias,
        grad_conv_in,
        grad_film_weight,
        grad_film_bias,
        grad_conv_out,
        grad_ln_gain,
        grad_qkv_weight,
        grad_out_weight,
        grad_text_weight,
    )


CHUNK = 256
HALF_ROWS = 10 * MAP_W


def quadrants(values):
    grid = values.reshape(2, MAP_H // 2, 2, MAP_W // 2, values.shape[-1])
    return [grid[a, :, b] for a in range(2) for b in range(2)]


def rejoin(parts):
    channels = parts[0].shape[-1]
    top = jnp.concatenate(
        [part.reshape(MAP_H // 2, 1, MAP_W // 2, channels) for part in parts[:2]], axis=1
    )
    low = jnp.concatenate(
        [part.reshape(MAP_H // 2, 1, MAP_W // 2, channels) for part in parts[2:]], axis=1
    )
    return jnp.concatenate([top, low], axis=0).reshape(MAP_H * MAP_W, channels)


def region_mean(parts, single, block_ones):
    rows = jnp.concatenate(
        [jnp.sum(part, axis=(0, 1), keepdims=True).reshape(1, -1) for part in parts], axis=0
    )
    rows = jnp.concatenate([rows, rows], axis=0)
    sums = jnp.dot(rows, block_ones, precision=highest, preferred_element_type=jnp.float32)
    quarter_count = (MAP_H * MAP_W // 4) * 32.0
    whole = jnp.sum(sums[:4], axis=0, keepdims=True) * (0.25 / quarter_count)
    return [jnp.where(single, whole, sums[i : i + 1] * (1.0 / quarter_count)) for i in range(4)]


def normalise(parts, single, block_ones):
    means = region_mean(parts, single, block_ones)
    centred = [part - mean[None] for part, mean in zip(parts, means)]
    spread = region_mean([part * part for part in centred], single, block_ones)
    rates = [lax.rsqrt(value + epsilon) for value in spread]
    return [part * rate[None] for part, rate in zip(centred, rates)], rates


def group_ones():
    row = lax.broadcasted_iota(jnp.int32, (CHUNK, CHUNK), 0) // 32
    col = lax.broadcasted_iota(jnp.int32, (CHUNK, CHUNK), 1) // 32
    return (row == col).astype(jnp.float32)


def put_shifts(values, single, taps, lanes):
    pixel = lax.broadcasted_iota(jnp.int32, values.shape, 0) % MAP_W
    for s in range(3):
        if s == 1:
            moved = values
        elif s == 2:
            moved = pltpu.roll(values, MAP_H * MAP_W - 1, 0)
            moved = jnp.where(
                (pixel != MAP_W - 1) & (single | (pixel != MAP_W // 2 - 1)), moved, 0.0
            )
        else:
            moved = pltpu.roll(values, 1, 0)
            moved = jnp.where((pixel != 0) & (single | (pixel != MAP_W // 2)), moved, 0.0)
        low = moved.astype(jnp.bfloat16)
        blank = jnp.zeros((MAP_W, values.shape[1]), jnp.bfloat16)
        taps[s, 0, 0:32, lanes] = blank
        taps[s, 0, 32:288, lanes] = low[0:256]
        taps[s, 0, 288:320, lanes] = jnp.where(single, moved[256:288], 0.0).astype(jnp.bfloat16)
        taps[s, 1, 0:32, lanes] = jnp.where(single, moved[224:256], 0.0).astype(jnp.bfloat16)
        taps[s, 1, 32:288, lanes] = low[256:512]
        taps[s, 1, 288:320, lanes] = blank


def tap_rows(taps, col_step, row_step, lanes):
    rows = taps[col_step, :, pl.ds(pl.multiple_of(row_step * MAP_W, MAP_W), 256), lanes]
    return rows.reshape(MAP_H * MAP_W, rows.shape[-1])


def own_first(start, core, width):
    return pl.ds(pl.multiple_of((start + core * 512) % 1024, width), width)


def forward_conv_kernel(finish, info, x, scale, shift, w_own, w_far, *refs):
    if finish:
        pixels, ln_gain, low_out, joined_out, normed_out, taps, acc = refs
    else:
        low_out, acc, taps = refs
    t = pl.program_id(0)
    core = info[0]
    single = info[1] == 1

    @pl.when(t == 0)
    def _():
        ones = group_ones()
        for start in range(0, 1024, CHUNK):
            lanes = pl.ds(start, CHUNK)
            parts = quadrants(x[:, lanes].astype(jnp.float32))
            normed, _ = normalise(parts, single, ones)
            pre = rejoin(normed) * scale[:, lanes] + shift[:, lanes]
            act = pre * jax.nn.sigmoid(pre)
            low_out[:, lanes] = act.astype(jnp.bfloat16)
            put_shifts(act, single, taps, own_first(start, core, CHUNK))

    rows = tap_rows(taps, t % 3, t // 3, slice(None))
    fresh = jnp.dot(rows[:, :512], w_own[0], preferred_element_type=jnp.float32)
    fresh += jnp.dot(rows[:, 512:], w_far[0], preferred_element_type=jnp.float32)

    @pl.when(t == 0)
    def _():
        acc[...] = fresh

    @pl.when(t > 0)
    def _():
        acc[...] += fresh

    if finish:

        @pl.when(t == 8)
        def _():
            joined = (pixels[...].astype(jnp.float32) + acc[...]) * inv_root_two
            joined_out[...] = joined
            centre = joined - jnp.mean(joined, axis=1, keepdims=True)
            rate = lax.rsqrt(jnp.mean(centre * centre, axis=1, keepdims=True) + epsilon)
            normed_out[...] = (centre * rate * ln_gain[...]).astype(jnp.bfloat16)


def whole(shape):
    return pl.BlockSpec(shape, lambda t, *_: (0,) * len(shape))


def forward_conv(info, x, scale, shift, w_own, w_far, extra=None):
    finish = extra is not None
    full = jax.ShapeDtypeStruct((512, 1024), jnp.float32)
    low = jax.ShapeDtypeStruct((512, 1024), jnp.bfloat16)
    field = whole((512, 1024))
    row = whole((1, 1024))
    tap = pl.BlockSpec((1, 512, 1024), lambda t, *_: (t, 0, 0))
    scratch = [pltpu.VMEM((3, 2, HALF_ROWS, 1024), jnp.bfloat16)]
    if finish:
        scratch += [pltpu.VMEM((512, 1024), jnp.float32)]
    return pl.pallas_call(
        functools.partial(forward_conv_kernel, finish),
        out_shape=(low, full, low) if finish else (low, full),
        grid_spec=pltpu.PrefetchScalarGridSpec(
            num_scalar_prefetch=1,
            grid=(9,),
            in_specs=[field, row, row, tap, tap] + ([field, row] if finish else []),
            out_specs=(field, field, field) if finish else (field, field),
            scratch_shapes=scratch,
        ),
        compiler_params=pltpu.CompilerParams(vmem_limit_bytes=56 << 20),
        name="forward_conv",
    )(info, x, scale, shift, w_own, w_far, *(extra or ()))


def to_wide(value, step):
    return lax.ppermute(value, "wide", [(i, i ^ step) for i in range(16)])


def to_far(value):
    return lax.ppermute(value, "narrow", [(0, 1), (1, 0)])


def gather_all(row):
    rows = row[None]
    rows = jnp.concatenate([rows, to_far(rows)])
    for step in (1, 2, 4, 8):
        rows = jnp.concatenate([rows, to_wide(rows, step)])
    return rows


def half_of(value, core, axis):
    size = value.shape[axis] // 2
    return lax.dynamic_slice_in_dim(value, core * size, size, axis)


def share_source(value_t, core):
    far = to_far(half_of(value_t, 1 - core, 0))
    pair = jnp.stack([half_of(value_t, core, 0), far])
    return (pair, to_wide(pair, 1), to_wide(pair, 2), to_wide(pair, 3))


def pair_of(value_t, core):
    far = to_far(half_of(value_t, 1 - core, 0))
    return jnp.concatenate([half_of(value_t, core, 0), far], axis=1)


def pair_body(
    pixels,
    layout,
    noise_group,
    cond_embed,
    text_embed,
    cotangent,
    gn_gain,
    gn_bias,
    conv_in,
    film_weight,
    film_bias,
    conv_out,
    ln_gain,
    qkv_weight,
    out_weight,
    text_weight,
):
    f32, bf16 = jnp.float32, jnp.bfloat16
    wide = lax.axis_index("wide")
    core = lax.axis_index("narrow")
    group_total = lax.axis_size("wide")

    conv_in_far = to_far(conv_in)
    vectors = jnp.concatenate([gn_gain, gn_bias, ln_gain, film_bias])
    vectors_far = to_far(vectors)
    low_vec = jnp.where(core == 0, vectors, vectors_far)
    high_vec = jnp.where(core == 0, vectors_far, vectors)

    def joined_vec(start, size):
        return jnp.concatenate([low_vec[start : start + size], high_vec[start : start + size]])

    gain_row = joined_vec(0, 512).astype(f32)[None]
    bias_row = joined_vec(512, 512).astype(f32)[None]
    ln_row = joined_vec(1024, 512).astype(f32)[None]
    film_bias_full = joined_vec(1536, 1024).astype(f32)
    conv_out_far = to_far(conv_out)

    facts = jnp.stack([noise_group[0], layout[0]])
    facts = jnp.pad(facts.astype(f32), (0, 126))
    early = gather_all(jnp.concatenate([cond_embed[0].astype(f32), facts]))
    cond_all = early[:, :1024]
    alike = jnp.sum((early[:, 1024] == facts[0]).astype(f32))
    weight = 1.0 / (group_total * alike)
    info = jnp.stack([core.astype(jnp.int32), layout[0]])
    layouts = early[:8, 1025].astype(jnp.int32)

    text_one = text_embed[0]
    text_sources = share_source(text_one.T, core)
    cot = cotangent[0]
    film_full = lax.all_gather(film_weight, "narrow", axis=0, tiled=True)
    qkv_full = lax.all_gather(qkv_weight, "narrow", axis=0, tiled=True)
    out_full = lax.all_gather(out_weight, "narrow", axis=0, tiled=True)
    text_full = lax.all_gather(text_weight, "narrow", axis=0, tiled=True)

    region_ids = region_ids_of(layout[0])
    field = pixels[0]
    condition = jax.nn.silu(cond_embed[0].astype(f32)).astype(bf16)
    film_out = jnp.dot(condition, film_full, preferred_element_type=f32) + film_bias_full
    film_scale = 1.0 + film_out[None, :1024]
    film_shift = film_out[None, 1024:]

    first_low, hidden_one = forward_conv(info, field, gain_row, bias_row, conv_in, conv_in_far)
    first_sources = share_source(first_low.T, core)
    second_low, joined, normed = forward_conv(
        info, hidden_one, film_scale, film_shift, conv_out, conv_out_far, (field, ln_row)
    )
    second_sources = share_source(second_low.T, core)

    attn_full = (ln_row[0], qkv_full, out_full, text_full)
    result, stored = attention_mid(normed, joined, text_one, region_ids, attn_full)
    output = result.astype(bf16)
    grad_joined, ln_term, grad_triple, grad_pair = attention_back(
        cot, joined, stored, attn_full
    )
    mixed = stored[5]
    grad_two = grad_joined * inv_root_two
    grad_two_low = grad_two.astype(bf16)

    pair_w = (weight * grad_pair).astype(bf16)
    pair_q = pair_w.reshape(TEXT_LEN, 2, 4, CHUNK).transpose(2, 0, 1, 3).reshape(4, TEXT_LEN, 512)
    two_w = (weight * grad_two).astype(bf16)
    two_q = two_w.reshape(512, 4, CHUNK).transpose(1, 0, 2)
    both_w = (weight * jnp.concatenate([grad_triple, cot.astype(f32)], axis=1)).astype(bf16)
    rows = jnp.concatenate(
        [film_scale, film_shift, gain_row, bias_row, ln_term[None], jnp.zeros((3, 1024), f32)]
    )

    big, _, input_grad, small_all = late(
        layouts,
        weight.reshape(1),
        pair_q,
        two_q,
        both_w,
        *text_sources,
        *second_sources,
        *first_sources,
        pair_of(normed.T, core),
        pair_of(mixed.T, core),
        grad_two_low,
        hidden_one,
        field,
        grad_joined,
        rows,
        conv_out,
        conv_out_far,
        conv_in,
        conv_in_far,
    )
    me = 2 * wide + core
    film_all = small_all[:, :2].reshape(32, 2048)
    cond_low = jax.nn.silu(cond_all).astype(bf16)[jnp.bitwise_xor(jnp.arange(32), me)]
    grad_film_weight = lax.dot_general(
        half_of(cond_low, core, 1),
        film_all.astype(bf16),
        (((0,), (0,)), ((), ())),
        preferred_element_type=f32,
    )
    small_sum = jnp.sum(small_all, axis=0)
    grad_film_bias = half_of(small_sum[:2].reshape(-1), core, 0)
    grad_gn_gain = half_of(small_sum[2], core, 0)
    grad_gn_bias = half_of(small_sum[3], core, 0)
    grad_ln_gain = half_of(small_sum[4], core, 0)
    tap = (1, 512, 1024)
    conv_shape = (9, 512, 1024)
    return (
        output[None],
        input_grad[None],
        grad_gn_gain,
        grad_gn_bias,
        widen(big, FIRST_IN, conv_shape, tap, 9, lambda k: (k, 0, 0)),
        grad_film_weight,
        grad_film_bias,
        widen(big, FIRST_OUT, conv_shape, tap, 9, lambda k: (k, 0, 0)),
        grad_ln_gain,
        widen(big, FIRST_ATTN, (512, 3072), tap[1:], 3, lambda k: (0, k)),
        widen(big, FIRST_ATTN + 3, (512, 1024), tap[1:], 1, lambda k: (0, 0)),
        widen(big, 0, (2048, 2048), tap[1:], 8, lambda k: (k // 2, k % 2)),
    )


def attention_mid(normed_low, joined, text_one, region_ids, attn_full):
    _, qkv_full, out_full, text_full = attn_full
    pixel_count, channels = joined.shape
    head_dim = channels // HEADS
    score_scale = head_dim ** (-0.5)
    triple = jnp.dot(normed_low, qkv_full, preferred_element_type=jnp.float32).astype(jnp.bfloat16)
    text_pair = jnp.dot(text_one, text_full, preferred_element_type=jnp.float32).astype(
        jnp.bfloat16
    )
    queries = triple[:, :channels].reshape(pixel_count, HEADS, head_dim)
    key_rows = jnp.concatenate(
        [triple[:, channels : 2 * channels], text_pair[:, :channels]], axis=0
    ).reshape(-1, HEADS, head_dim)
    value_rows = jnp.concatenate(
        [triple[:, 2 * channels :], text_pair[:, channels:]], axis=0
    ).reshape(-1, HEADS, head_dim)
    allowed = allowed_keys(region_ids)
    masked = jnp.where(
        allowed[None],
        jnp.einsum("phd,jhd->hpj", queries, key_rows, preferred_element_type=jnp.float32)
        * score_scale,
        masked_score,
    )
    row_peak = jnp.max(masked, axis=2, keepdims=True)
    exponent = jnp.exp(masked - row_peak)
    exp_total = jnp.sum(exponent, axis=2, keepdims=True)
    attn_probs = exponent / exp_total
    log_total = row_peak + jnp.log(exp_total)
    mixed = (
        jnp.einsum(
            "hpj,jhd->phd",
            attn_probs.astype(jnp.bfloat16),
            value_rows,
            preferred_element_type=jnp.float32,
        )
        .reshape(pixel_count, channels)
        .astype(jnp.bfloat16)
    )
    result = joined + jnp.dot(mixed, out_full, preferred_element_type=jnp.float32)
    return (result, (normed_low, queries, key_rows, value_rows, log_total, mixed, allowed))


def attention_back(grad_result, joined, stored, attn_full):
    gain_row, qkv_full, out_full, text_full = attn_full
    normed_low, queries, key_rows, value_rows, log_total, mixed, allowed = stored
    pixel_count, channels = joined.shape
    head_dim = channels // HEADS
    score_scale = head_dim ** (-0.5)
    grad_mixed = (
        jnp.einsum("pd,cd->pc", grad_result, out_full, preferred_element_type=jnp.float32)
        .astype(jnp.bfloat16)
        .reshape(pixel_count, HEADS, head_dim)
    )
    masked = jnp.where(
        allowed[None],
        jnp.einsum("phd,jhd->hpj", queries, key_rows, preferred_element_type=jnp.float32)
        * score_scale,
        masked_score,
    )
    attn_probs = jnp.exp(masked - log_total)
    grad_probs = jnp.einsum(
        "phd,jhd->hpj", grad_mixed, value_rows, preferred_element_type=jnp.float32
    )
    grad_values = jnp.einsum(
        "hpj,phd->jhd",
        attn_probs.astype(jnp.bfloat16),
        grad_mixed,
        preferred_element_type=jnp.float32,
    )
    row_inner = jnp.sum(attn_probs * grad_probs, axis=2, keepdims=True)
    grad_scores = (attn_probs * (grad_probs - row_inner)).astype(jnp.bfloat16)
    grad_queries = (
        jnp.einsum("hpj,jhd->phd", grad_scores, key_rows, preferred_element_type=jnp.float32)
        * score_scale
    )
    grad_keys = (
        jnp.einsum("hpj,phd->jhd", grad_scores, queries, preferred_element_type=jnp.float32)
        * score_scale
    )
    grad_triple = jnp.concatenate(
        [
            grad_queries.reshape(pixel_count, channels),
            grad_keys[:pixel_count].reshape(pixel_count, channels),
            grad_values[:pixel_count].reshape(pixel_count, channels),
        ],
        axis=1,
    )
    grad_pair = jnp.concatenate(
        [
            grad_keys[pixel_count:].reshape(-1, channels),
            grad_values[pixel_count:].reshape(-1, channels),
        ],
        axis=1,
    )
    grad_normed = jnp.einsum(
        "pk,ck->pc", grad_triple.astype(jnp.bfloat16), qkv_full, preferred_element_type=jnp.float32
    )
    _, norm_back = jax.vjp(layer_norm, joined, gain_row)
    grad_joined_norm, term_gain = norm_back(grad_normed)
    return (grad_result.astype(jnp.float32) + grad_joined_norm, term_gain, grad_triple, grad_pair)


MESH = pl.DeviceIdType.MESH
CHUNKS = 30
FIRST_OUT, FIRST_ATTN, FIRST_IN = 8, 17, 21


def late_kernel(
    layouts, weight,
    pair_q, two_q, both_w, text0, text1, text2, text3, second0, second1, second2, second3,
    first0, first1, first2, first3, normed_t, mixed_t, two_low_in, hidden_in, field_in,
    passed_in, rows_in, out_own, out_far, in_own, in_far,
    big, both_far, input_grad, small_out,
    held, total, cross, taps, sources, pair_slots, two_slots, hid_slots, rhs, rs_in,
    weights, acc, wide_field, field, two_low, hidden_low, hidden_q, rows, small,
    s1s, s1r, s2s, s2r, s3s, s3r, xs, xr, ys, yr, d0s, d0r, d1s, d1r, own_sem,
    pair_s, pair_r, two_s, two_r, hid_s, hid_r, both_s, both_r, rs_s, rs_r, small_s, small_r,
    text_sem, source_sem, rhs_sem, load_sem, weight_sem, keep_sem,
):
    f32, bf16 = jnp.float32, jnp.bfloat16
    w = lax.axis_index("wide")
    c = lax.axis_index("narrow")
    p = w % 4
    z = w // 4
    wx = w + 1 - 2 * (w % 2)
    wy = w + 2 - 4 * ((w // 2) % 2)
    wd = 4 * z + 3 - p
    wz = w + 4 - 8 * (z % 2)
    wm = (3 - z) * 4 + p
    px = p + 1 - 2 * (p % 2)
    py = p + 2 - 4 * (p // 2)
    pd = 3 - p
    steps = ((wx, px), (wy, py), (wd, pd))
    is_mid = (z == 1) | (z == 2)
    is_end = (z == 0) | (z == 3)
    single = layouts[0] == 1

    bar = pltpu.get_barrier_semaphore()
    for t in (wx, wy, wd, wz):
        pl.semaphore_signal(bar, inc=1, device_id=(t, c), device_id_type=MESH)
    pl.semaphore_signal(bar, inc=1, device_id=(w, 1 - c), device_id_type=MESH)

    @pl.when(is_mid)
    def _():
        pl.semaphore_signal(bar, inc=1, device_id=(wm, c), device_id_type=MESH)
        pl.semaphore_wait(bar, 6)

    @pl.when(is_end)
    def _():
        pl.semaphore_wait(bar, 5)

    def remote(src, dst, ss, rs, t):
        return pltpu.make_async_remote_copy(
            src_ref=src, dst_ref=dst, send_sem=ss, recv_sem=rs, device_id=(t, c), device_id_type=MESH
        )

    def across(src, dst, ss, rs):
        return pltpu.make_async_remote_copy(
            src_ref=src, dst_ref=dst, send_sem=ss, recv_sem=rs, device_id=(w, 1 - c),
            device_id_type=MESH,
        )

    def local(src, dst, sem):
        return pltpu.make_async_copy(src, dst, sem)

    def quarter_copies(quarters, slots, ss, rs):
        sends = [
            remote(quarters.at[q], slots.at[2 * (i + 1)], ss.at[i], rs.at[i], t)
            for i, (t, q) in enumerate(steps)
        ]
        sends.append(across(quarters.at[p], slots.at[1], ss.at[3], rs.at[3]))
        passes = [
            across(slots.at[2 * i + 2], slots.at[2 * i + 3], ss.at[4 + i], rs.at[4 + i])
            for i in range(3)
        ]
        return sends, passes

    def start_quarters(quarters, slots, ss, rs, sem):
        sends, _ = quarter_copies(quarters, slots, ss, rs)
        for copy in (sends[2], sends[0], sends[1], sends[3]):
            copy.start()
        local(quarters.at[p], slots.at[0], sem).start()

    def pass_quarters(quarters, slots, ss, rs):
        sends, passes = quarter_copies(quarters, slots, ss, rs)
        for i in range(3):
            sends[i].wait_recv()
            passes[i].start()

    def finish_quarters(quarters, slots, ss, rs, sem):
        sends, passes = quarter_copies(quarters, slots, ss, rs)
        for copy in sends:
            copy.wait_send()
        sends[3].wait_recv()
        for copy in passes:
            copy.wait()
        local(quarters.at[p], slots.at[0], sem).wait()

    def column(q):
        return pl.ds(pl.multiple_of(q * CHUNK, CHUNK), CHUNK)

    def up(k):
        return remote(held.at[k], total.at[k], s1s.at[k], s1r.at[k], wz)

    def over(k):
        return remote(held.at[k], cross.at[k], s2s.at[k], s2r.at[k], wm)

    def down(k):
        return remote(total.at[k], total.at[k], s3s.at[k], s3r.at[k], wz)

    def to_x(k, q):
        return remote(total.at[k], big.at[k, :, column(q)], xs.at[k], xr.at[k], wx)

    def to_y(k, q):
        return remote(total.at[k], big.at[k, :, column(q)], ys.at[k], yr.at[k], wy)

    def on_x(k, q):
        part = big.at[k, pl.ds(0, 256), column(q)]
        return remote(part, part, d0s.at[k], d0r.at[k], wx)

    def on_y(k, q):
        part = big.at[k, pl.ds(256, 256), column(q)]
        return remote(part, part, d1s.at[k], d1r.at[k], wy)

    def own(k):
        return local(total.at[k], big.at[k, :, column(p)], own_sem.at[k])

    def offer(k):
        @pl.when(is_end)
        def _():
            up(k).start()

    def tick(k):
        @pl.when(is_mid & (k < CHUNKS))
        def _():
            up(k).wait_recv()
            held[k] = (held[k].astype(f32) + total[k].astype(f32)).astype(bf16)
            over(k).start()

        kb = k - 1

        @pl.when((kb >= 0) & (kb < CHUNKS))
        def _():
            @pl.when(is_mid)
            def _():
                over(kb).wait_recv()
                total[kb] = (held[kb].astype(f32) + cross[kb].astype(f32)).astype(bf16)
                down(kb).start()

            @pl.when(is_end)
            def _():
                down(kb).wait_recv()

            to_x(kb, p).start()
            to_y(kb, p).start()
            own(kb).start()

        kc = k - 2

        @pl.when((kc >= 0) & (kc < CHUNKS))
        def _():
            to_x(kc, px).wait_recv()
            to_y(kc, py).wait_recv()
            on_x(kc, py).start()
            on_y(kc, px).start()

        kd = k - 3

        @pl.when((kd >= 0) & (kd < CHUNKS))
        def _():
            on_x(kd, pd).wait_recv()
            on_y(kd, pd).wait_recv()

    start_quarters(pair_q, pair_slots, pair_s, pair_r, keep_sem.at[0])
    across(both_w, both_far, both_s, both_r).start()
    start_quarters(two_q, two_slots, two_s, two_r, keep_sem.at[1])

    text = (text0, text1, text2, text3)

    def text_loads(i):
        slot = 2 * (i % 2)
        rows_i = pl.ds(pl.multiple_of(i * 512, 512), 512)
        return [
            local(
                text[j].at[e, rows_i],
                sources.at[slot + j // 2, :, pl.ds(TEXT_LEN * (2 * (j % 2) + e), TEXT_LEN)],
                text_sem.at[i % 2, 2 * j + e],
            )
            for j in range(4)
            for e in range(2)
        ]

    for copy in text_loads(0):
        copy.start()
    loads = [
        local(normed_t, weights.at[0, 0], load_sem.at[0]),
        local(mixed_t, weights.at[0, 1], load_sem.at[1]),
        local(hidden_in, wide_field, load_sem.at[2]),
        local(field_in, field, load_sem.at[3]),
        local(two_low_in, two_low, load_sem.at[4]),
        local(rows_in, rows, load_sem.at[5]),
    ]
    for copy in loads:
        copy.start()
    pass_quarters(pair_q, pair_slots, pair_s, pair_r)
    finish_quarters(pair_q, pair_slots, pair_s, pair_r, keep_sem.at[0])

    def text_step(i, _):
        @pl.when(i < 3)
        def _():
            for copy in text_loads(i + 1):
                copy.start()

        for copy in text_loads(i):
            copy.wait()
        slot = 2 * (i % 2)
        right = pair_slots[...].reshape(8 * TEXT_LEN, 2 * CHUNK)
        value = jnp.dot(sources[slot], right[:512], preferred_element_type=f32)
        value += jnp.dot(sources[slot + 1], right[512:], preferred_element_type=f32)
        value = value.astype(bf16)
        held[2 * i] = value[:, :CHUNK]
        held[2 * i + 1] = value[:, CHUNK:]
        offer(2 * i)
        offer(2 * i + 1)
        return 0

    lax.fori_loop(0, 4, text_step, 0)

    def source_loads(parts):
        return [
            local(parts[j].at[e], sources.at[2 * j + e], source_sem.at[2 * j + e])
            for j in range(4)
            for e in range(2)
        ]

    second_loads = source_loads((second0, second1, second2, second3))
    for copy in second_loads:
        copy.start()

    across(both_w, both_far, both_s, both_r).wait()
    loads[0].wait()
    loads[1].wait()

    def rhs_loads(q, j, slot):
        col = pl.ds(pl.multiple_of(j * 1024 + q * CHUNK, CHUNK), CHUNK)
        return (
            local(both_w.at[:, col], rhs.at[slot, pl.ds(0, 512)], rhs_sem.at[slot, 0]),
            local(both_far.at[:, col], rhs.at[slot, pl.ds(512, 512)], rhs_sem.at[slot, 1]),
        )

    staged = (hidden_q, held, held, held)
    staged_base = (0, FIRST_IN, FIRST_IN + 4, FIRST_ATTN)

    def rs_copy(m, j):
        return remote(
            staged[m].at[staged_base[m] + j], rs_in.at[m, j], rs_s.at[m, j], rs_r.at[m, j], steps[m][0]
        )

    order = (2, 0, 1, 3)
    quarter_of = (px, py, pd, p)
    for copy in rhs_loads(quarter_of[2], 0, 0):
        copy.start()
    for place, m in enumerate(order):

        def attn_step(j, _, m=m, place=place):
            slot = j % 2

            @pl.when(j < 3)
            def _():
                for copy in rhs_loads(quarter_of[m], j + 1, 1 - slot):
                    copy.start()

            if place < 3:

                @pl.when(j == 3)
                def _():
                    for copy in rhs_loads(quarter_of[order[place + 1]], 0, 1 - slot):
                        copy.start()

            for copy in rhs_loads(quarter_of[m], j, slot):
                copy.wait()
            left = weights[0, j // 3]
            value = jnp.dot(left, rhs[slot], preferred_element_type=f32)
            staged[m][staged_base[m] + j] = value.astype(bf16)
            if m < 3:
                rs_copy(m, j).start()
            return 0

        lax.fori_loop(0, 4, attn_step, 0)
        if place == 1:
            pass_quarters(two_q, two_slots, two_s, two_r)
            tick(0)
        if place == 3:
            tick(1)

    def conv_term_taps(slots):
        for i in range(8):
            put_shifts(slots[i].astype(f32), layouts[i] == 1, taps.at[i], slice(None))

    def conv_term_loop(base, first_tick):
        def step(t, _):
            value = jnp.zeros((512, CHUNK), f32)
            for i in range(8):
                part = tap_rows(taps.at[i], 2 - t % 3, 2 - t // 3, slice(None))
                value += jnp.dot(sources[i], part, preferred_element_type=f32)
            held[base + t] = value.astype(bf16)
            offer(base + t)

            @pl.when(t % 3 == 2)
            def _():
                tick(first_tick + t // 3)

            return 0

        lax.fori_loop(0, 9, step, 0)

    finish_quarters(two_q, two_slots, two_s, two_r, keep_sem.at[1])
    conv_term_taps(two_slots)
    for copy in second_loads:
        copy.wait()
    conv_term_loop(FIRST_OUT, 2)
    first_loads = source_loads((first0, first1, first2, first3))
    for copy in first_loads:
        copy.start()

    def conv_back(grad, w_own, w_far, first_tick):
        def weight_loads(t):
            slot = t % 2
            return (
                local(w_own.at[t], weights.at[slot, 0], weight_sem.at[slot, 0]),
                local(w_far.at[t], weights.at[slot, 1], weight_sem.at[slot, 1]),
            )

        for copy in weight_loads(0):
            copy.start()
        for i in range(4):
            put_shifts(
                grad[:, i * CHUNK : (i + 1) * CHUNK].astype(f32), single, taps.at[i], slice(None)
            )
        acc[...] = jnp.zeros((512, 1024), f32)
        last = (((1,), (1,)), ((), ()))

        def step(t, _):
            @pl.when(t < 8)
            def _():
                for copy in weight_loads(t + 1):
                    copy.start()

            for copy in weight_loads(t):
                copy.wait()
            part = jnp.concatenate(
                [tap_rows(taps.at[i], 2 - t % 3, 2 - t // 3, slice(None)) for i in range(4)], axis=1
            )
            for side in range(2):
                acc[:, side * 512 : side * 512 + 512] += lax.dot_general(
                    part, weights[t % 2, side], last, preferred_element_type=f32
                )

            @pl.when(t % 3 == 2)
            def _():
                tick(first_tick + t // 3)

            return 0

        lax.fori_loop(0, 9, step, 0)

    def norm_back(x, at, put):
        ones = group_ones()

        def block(i, _):
            lanes = column(i)
            parts = quadrants(x[:, lanes].astype(f32))
            normed, rates = normalise(parts, single, ones)
            gains = rows[at : at + 1, lanes]
            shift = rows[at + 1 : at + 2, lanes]
            pre = [part * gains[None] + shift[None] for part in normed]
            grads = quadrants(acc[:, own_first(i * CHUNK, c, CHUNK)])
            sig = [jax.nn.sigmoid(part) for part in pre]
            grads = [g * s * (1.0 + v * (1.0 - s)) for g, s, v in zip(grads, sig, pre)]
            small[pl.ds(2 * w + c, 1), at : at + 1, lanes] = sum(
                jnp.sum(g * n, axis=(0, 1), keepdims=True) for g, n in zip(grads, normed)
            )
            small[pl.ds(2 * w + c, 1), at + 1 : at + 2, lanes] = sum(
                jnp.sum(g, axis=(0, 1), keepdims=True) for g in grads
            )
            grads = [g * gains[None] for g in grads]
            mean = region_mean(grads, single, ones)
            slope = region_mean([g * n for g, n in zip(grads, normed)], single, ones)
            put(
                i,
                lanes,
                rejoin(
                    [
                        r[None] * (g - m[None] - n * s[None])
                        for r, g, m, n, s in zip(rates, grads, mean, normed, slope)
                    ]
                ),
            )
            return 0

        lax.fori_loop(0, 4, block, 0)

    loads[4].wait()
    loads[5].wait()
    conv_back(two_low, out_own, out_far, 5)
    loads[2].wait()

    for m in range(3):
        for j in range(4):
            rs_copy(m, j).wait_send()

    def put_hidden(i, lanes, value):
        hidden_low[:, lanes] = value.astype(bf16)
        hidden_q[i] = (value * weight[0]).astype(bf16)

    norm_back(wide_field, 0, put_hidden)
    start_quarters(hidden_q, hid_slots, hid_s, hid_r, keep_sem.at[2])
    pass_load = local(passed_in, wide_field, keep_sem.at[3])
    pass_load.start()

    for m in range(3):
        for j in range(4):
            rs_copy(m, j).wait_recv()

    def attn_sum(j, _):
        k = FIRST_ATTN + j
        value = held[k].astype(f32)
        for m in range(3):
            value += rs_in[m, j].astype(f32)
        held[k] = value.astype(bf16)
        offer(k)
        return 0

    lax.fori_loop(0, 4, attn_sum, 0)
    tick(8)

    conv_back(hidden_low, in_own, in_far, 9)
    loads[3].wait()
    pass_load.wait()

    def put_input(i, lanes, value):
        two_low[:, lanes] = (value + wide_field[:, lanes] * inv_root_two).astype(bf16)

    norm_back(field, 2, put_input)
    keep = local(two_low, input_grad, keep_sem.at[4])
    keep.start()
    me = 2 * w + c
    small[pl.ds(me, 1), 4:8] = rows[4:8][None]
    small[pl.ds(me, 1)] = small[pl.ds(me, 1)] * weight[0]
    pass_quarters(hidden_q, hid_slots, hid_s, hid_r)
    tick(12)
    finish_quarters(hidden_q, hid_slots, hid_s, hid_r, keep_sem.at[2])
    conv_term_taps(hid_slots)
    for copy in first_loads:
        copy.wait()

    def small_rows(start, count):
        return small.at[pl.ds(start, count)]

    def small_copy(r):
        if r == 0:
            part = small_rows(me, 1)
            return across(part, part, small_s.at[0], small_r.at[0])
        if r == 1:
            part = small_rows(2 * w, 2)
            return remote(part, part, small_s.at[1], small_r.at[1], wx)
        if r == 2:
            part = small_rows(4 * (w // 2), 4)
            return remote(part, part, small_s.at[2], small_r.at[2], wy)
        if r == 3:
            part = small_rows(8 * z, 8)
            return remote(part, part, small_s.at[3], small_r.at[3], wz)
        if r == 4:
            part = small_rows(16 * (z // 2), 16)
            return remote(part, part, small_s.at[4], small_r.at[4], wm)
        part = small_rows(16 * (1 - z // 2), 16)
        return remote(part, part, small_s.at[5], small_r.at[5], wz)

    def small_arrival(r):
        if r == 0:
            part = small_rows(2 * w + 1 - c, 1)
            return across(part, part, small_s.at[0], small_r.at[0])
        if r == 1:
            part = small_rows(2 * wx, 2)
            return remote(part, part, small_s.at[1], small_r.at[1], wx)
        if r == 2:
            part = small_rows(4 * (wy // 2), 4)
            return remote(part, part, small_s.at[2], small_r.at[2], wy)
        if r == 3:
            part = small_rows(8 * (wz // 4), 8)
            return remote(part, part, small_s.at[3], small_r.at[3], wz)
        if r == 4:
            part = small_rows(16 * (wm // 8), 16)
            return remote(part, part, small_s.at[4], small_r.at[4], wm)
        part = small_rows(16 * (1 - z // 2), 16)
        return remote(part, part, small_s.at[5], small_r.at[5], wz)

    small_copy(0).start()
    conv_term_loop(FIRST_IN, 13)
    for r in range(4):
        small_arrival(r).wait_recv()
        if r < 3:
            small_copy(r + 1).start()
        tick(16 + r)

    @pl.when(is_mid)
    def _():
        small_copy(4).start()
        small_arrival(4).wait_recv()
        small_copy(5).start()

    def rest(k, _):
        tick(k)
        return 0

    lax.fori_loop(20, CHUNKS + 3, rest, 0)

    @pl.when(is_end)
    def _():
        small_arrival(5).wait_recv()

    for r in range(4):
        small_copy(r).wait_send()

    @pl.when(is_mid)
    def _():
        small_copy(4).wait_send()
        small_copy(5).wait_send()

    small_keep = local(small, small_out, keep_sem.at[5])
    small_keep.start()

    def finish(k, _):
        @pl.when(is_end)
        def _():
            up(k).wait_send()

        @pl.when(is_mid)
        def _():
            over(k).wait_send()
            down(k).wait_send()

        to_x(k, p).wait_send()
        to_y(k, p).wait_send()
        on_x(k, py).wait_send()
        on_y(k, px).wait_send()
        own(k).wait()
        return 0

    lax.fori_loop(0, CHUNKS, finish, 0)
    keep.wait()
    small_keep.wait()


def late(layouts, weight, *operands):
    bf16, f32 = jnp.bfloat16, jnp.float32
    any_spec = pl.BlockSpec(memory_space=pl.ANY)
    smem = pl.BlockSpec(memory_space=pltpu.SMEM)
    dma = pltpu.SemaphoreType.DMA
    chunks = pltpu.VMEM((CHUNKS, 512, CHUNK), bf16)
    map_low = pltpu.VMEM((512, 1024), bf16)
    map_full = pltpu.VMEM((512, 1024), f32)
    slots = pltpu.VMEM((8, 512, CHUNK), bf16)
    return pl.pallas_call(
        late_kernel,
        out_shape=(
            jax.ShapeDtypeStruct((CHUNKS, 512, 1024), bf16),
            jax.ShapeDtypeStruct((512, 4096), bf16),
            jax.ShapeDtypeStruct((512, 1024), bf16),
            jax.ShapeDtypeStruct((32, 8, 1024), f32),
        ),
        in_specs=[smem, smem] + [any_spec] * len(operands),
        out_specs=[any_spec] * 4,
        scratch_shapes=[
            chunks, chunks, chunks,
            pltpu.VMEM((8, 3, 2, HALF_ROWS, CHUNK), bf16),
            pltpu.VMEM((8, 512, 512), bf16),
            pltpu.VMEM((8, TEXT_LEN, 2 * CHUNK), bf16),
            slots, slots,
            pltpu.VMEM((2, 1024, CHUNK), bf16),
            pltpu.VMEM((3, 4, 512, CHUNK), bf16),
            pltpu.VMEM((2, 2, 512, 1024), bf16),
            map_full, map_full, map_low, map_low, map_low,
            pltpu.VMEM((4, 512, CHUNK), bf16),
            pltpu.VMEM((8, 1024), f32),
            pltpu.VMEM((32, 8, 1024), f32),
        ]
        + [dma((CHUNKS,))] * 15
        + [dma((7,))] * 6
        + [dma, dma, dma((3, 4)), dma((3, 4)), dma((6,)), dma((6,))]
        + [dma((2, 8)), dma((8,)), dma((2, 2)), dma((6,)), dma((2, 2)), dma((6,))],
        compiler_params=pltpu.CompilerParams(
            collective_id=0, has_side_effects=True, vmem_limit_bytes=62 << 20
        ),
        name="late_terms",
    )(layouts, weight, *operands)


def widen_kernel(low, out):
    out[...] = low[...].reshape(out.shape).astype(jnp.float32)


def widen(big, first, shape, block, count, where):
    return pl.pallas_call(
        widen_kernel,
        out_shape=jax.ShapeDtypeStruct(shape, jnp.float32),
        grid=(count,),
        in_specs=[pl.BlockSpec((1, 512, 1024), lambda k: (first + k, 0, 0))],
        out_specs=pl.BlockSpec(block, where),
        name="widen",
    )(big)


def solution(mesh):
    fits = mesh.shape["wide"] == 16 and mesh.shape["narrow"] == 2
    body = pair_body if fits else plain_body
    placed = (
        P(("wide", "narrow"), None, None),
        P(("wide", "narrow")),
        P(("wide", "narrow")),
        P(("wide", "narrow"), None),
        P(("wide", "narrow"), None, None),
        P(("wide", "narrow"), None, None),
        P("narrow"),
        P("narrow"),
        P(None, "narrow", None),
        P("narrow", None),
        P("narrow"),
        P(None, "narrow", None),
        P("narrow"),
        P("narrow", None),
        P("narrow", None),
        P("narrow", None),
    )
    return jax.shard_map(
        body,
        mesh=mesh,
        in_specs=placed,
        out_specs=(
            P(("wide", "narrow"), None, None),
            P(("wide", "narrow"), None, None),
            P("narrow"),
            P("narrow"),
            P(None, "narrow", None),
            P("narrow", None),
            P("narrow"),
            P(None, "narrow", None),
            P("narrow"),
            P("narrow", None),
            P("narrow", None),
            P("narrow", None),
        ),
        check_vma=False,
    )
```

```python
import functools

import jax
import jax.numpy as jnp
from jax import lax
from jax.experimental import pallas as pl
from jax.experimental.pallas import tpu as pltpu
from jax.sharding import PartitionSpec as P

NORM_GROUPS = 32
HEADS = 8
TEXT_LEN = 128
MAP_H = 16
MAP_W = 32


highest = lax.Precision.HIGHEST
epsilon = 1e-05
inv_root_two = 0.7071067811865476
masked_score = -1e30


def region_ids_of(layout_value):
    position = jnp.arange(MAP_H * MAP_W, dtype=jnp.int32)
    quarter = 2 * (position // MAP_W >= MAP_H // 2).astype(jnp.int32) + (
        position % MAP_W >= MAP_W // 2
    ).astype(jnp.int32)
    return jnp.where(layout_value == 1, jnp.zeros_like(quarter), quarter)


def tap_validity(region_ids):
    code_grid = region_ids.reshape(MAP_H, MAP_W)
    padded = jnp.pad(code_grid, 1, constant_values=-1)
    found = []
    for row_step in (-1, 0, 1):
        for col_step in (-1, 0, 1):
            neighbour = padded[
                1 + row_step : 1 + row_step + MAP_H, 1 + col_step : 1 + col_step + MAP_W
            ]
            found.append((neighbour == code_grid).reshape(-1))
    return jnp.stack(found)


def unfold(values, tap_valid):
    channels = values.shape[-1]
    padded = jnp.pad(values.reshape(MAP_H, MAP_W, channels), ((1, 1), (1, 1), (0, 0)))
    pieces = []
    tap_index = 0
    for row_step in (-1, 0, 1):
        for col_step in (-1, 0, 1):
            neighbour = padded[
                1 + row_step : 1 + row_step + MAP_H, 1 + col_step : 1 + col_step + MAP_W
            ].reshape(MAP_H * MAP_W, channels)
            pieces.append(
                jnp.where(tap_valid[tap_index][:, None], neighbour, jnp.zeros_like(neighbour))
            )
            tap_index += 1
    return jnp.concatenate(pieces, axis=1)


def fold_back(grad_cols, tap_valid):
    channels = grad_cols.shape[1] // 9
    start_point = jnp.zeros((grad_cols.shape[0], channels), jnp.float32)
    unfolded, pullback = jax.vjp(lambda field: unfold(field, tap_valid), start_point)
    return pullback(grad_cols)[0]


def group_norm(values, members):
    pixel_count, channels = values.shape
    grouped = values.reshape(pixel_count, NORM_GROUPS, channels // NORM_GROUPS)
    counts = jnp.maximum(jnp.sum(members, axis=0) * (channels // NORM_GROUPS), 1.0)
    region_sums = jnp.einsum("pr,pg->rg", members, jnp.sum(grouped, axis=2), precision=highest)
    pixel_means = jnp.einsum("pr,rg->pg", members, region_sums / counts[:, None], precision=highest)
    centred = grouped - pixel_means[:, :, None]
    squares = jnp.einsum(
        "pr,pg->rg", members, jnp.sum(centred * centred, axis=2), precision=highest
    )
    spreads = jnp.einsum(
        "pr,rg->pg", members, lax.rsqrt(squares / counts[:, None] + epsilon), precision=highest
    )
    return (centred * spreads[:, :, None]).reshape(pixel_count, channels)


def layer_norm(field, gain_in):
    centre = field - jnp.mean(field, axis=1, keepdims=True)
    return centre * lax.rsqrt(jnp.mean(centre * centre, axis=1, keepdims=True) + epsilon) * gain_in


def first_block(field, gain_in, bias_in, members):
    return jax.nn.silu(group_norm(field, members) * gain_in + bias_in)


def mid_block(hidden_in, film_in, members):
    channels = hidden_in.shape[1]
    return jax.nn.silu(
        group_norm(hidden_in, members) * (1.0 + film_in[:channels]) + film_in[channels:]
    )


def residual_front(field, members, tap_valid, condition, weights_full):
    gain_full, bias_full, conv_first, film_full, film_bias_full, conv_second = weights_full
    channels = field.shape[1]
    first_act, first_back = jax.vjp(
        lambda field_in, gain_in, bias_in: first_block(field_in, gain_in, bias_in, members),
        field,
        gain_full.astype(jnp.float32),
        bias_full.astype(jnp.float32),
    )
    first_low = first_act.astype(jnp.bfloat16)
    first_cols = unfold(first_low, tap_valid)
    hidden_one = jnp.dot(
        first_cols, conv_first.reshape(-1, channels), preferred_element_type=jnp.float32
    )
    film_out = jnp.dot(
        condition, film_full, preferred_element_type=jnp.float32
    ) + film_bias_full.astype(jnp.float32)
    second_act, mid_back = jax.vjp(
        lambda hidden_in, film_in: mid_block(hidden_in, film_in, members), hidden_one, film_out
    )
    second_low = second_act.astype(jnp.bfloat16)
    second_cols = unfold(second_low, tap_valid)
    return (first_cols, second_cols, first_back, mid_back)


def allowed_keys(region_ids):
    same_region = region_ids[:, None] == region_ids[None, :]
    return jnp.concatenate(
        [same_region, jnp.ones((region_ids.shape[0], TEXT_LEN), dtype=jnp.bool_)], axis=1
    )


def attention_forward(joined, text_one, region_ids, attn_full):
    gain_full, qkv_full, out_full, text_full = attn_full
    pixel_count, channels = joined.shape
    head_dim = channels // HEADS
    score_scale = head_dim ** (-0.5)
    normed_low = layer_norm(joined, gain_full.astype(jnp.float32)).astype(jnp.bfloat16)
    triple = jnp.dot(normed_low, qkv_full, preferred_element_type=jnp.float32).astype(jnp.bfloat16)
    text_pair = jnp.dot(text_one, text_full, preferred_element_type=jnp.float32).astype(
        jnp.bfloat16
    )
    queries = triple[:, :channels].reshape(pixel_count, HEADS, head_dim)
    key_rows = jnp.concatenate(
        [triple[:, channels : 2 * channels], text_pair[:, :channels]], axis=0
    ).reshape(-1, HEADS, head_dim)
    value_rows = jnp.concatenate(
        [triple[:, 2 * channels :], text_pair[:, channels:]], axis=0
    ).reshape(-1, HEADS, head_dim)
    allowed = allowed_keys(region_ids)
    masked = jnp.where(
        allowed[None],
        jnp.einsum("phd,jhd->hpj", queries, key_rows, preferred_element_type=jnp.float32)
        * score_scale,
        masked_score,
    )
    row_peak = jnp.max(masked, axis=2, keepdims=True)
    exponent = jnp.exp(masked - row_peak)
    exp_total = jnp.sum(exponent, axis=2, keepdims=True)
    attn_probs = exponent / exp_total
    log_total = row_peak + jnp.log(exp_total)
    mixed = (
        jnp.einsum(
            "hpj,jhd->phd",
            attn_probs.astype(jnp.bfloat16),
            value_rows,
            preferred_element_type=jnp.float32,
        )
        .reshape(pixel_count, channels)
        .astype(jnp.bfloat16)
    )
    result = joined + jnp.dot(mixed, out_full, preferred_element_type=jnp.float32)
    return (result, (normed_low, queries, key_rows, value_rows, log_total, mixed, allowed))


def attention_backward(grad_result, joined, text_one, stored, attn_full):
    gain_full, qkv_full, out_full, text_full = attn_full
    normed_low, queries, key_rows, value_rows, log_total, mixed, allowed = stored
    pixel_count, channels = joined.shape
    head_dim = channels // HEADS
    score_scale = head_dim ** (-0.5)
    grad_mixed = (
        jnp.einsum("pd,cd->pc", grad_result, out_full, preferred_element_type=jnp.float32)
        .astype(jnp.bfloat16)
        .reshape(pixel_count, HEADS, head_dim)
    )
    masked = jnp.where(
        allowed[None],
        jnp.einsum("phd,jhd->hpj", queries, key_rows, preferred_element_type=jnp.float32)
        * score_scale,
        masked_score,
    )
    attn_probs = jnp.exp(masked - log_total)
    grad_probs = jnp.einsum(
        "phd,jhd->hpj", grad_mixed, value_rows, preferred_element_type=jnp.float32
    )
    grad_values = jnp.einsum(
        "hpj,phd->jhd",
        attn_probs.astype(jnp.bfloat16),
        grad_mixed,
        preferred_element_type=jnp.float32,
    )
    row_inner = jnp.sum(attn_probs * grad_probs, axis=2, keepdims=True)
    grad_scores = (attn_probs * (grad_probs - row_inner)).astype(jnp.bfloat16)
    grad_queries = (
        jnp.einsum("hpj,jhd->phd", grad_scores, key_rows, preferred_element_type=jnp.float32)
        * score_scale
    )
    grad_keys = (
        jnp.einsum("hpj,phd->jhd", grad_scores, queries, preferred_element_type=jnp.float32)
        * score_scale
    )
    grad_triple = jnp.concatenate(
        [
            grad_queries.reshape(pixel_count, channels),
            grad_keys[:pixel_count].reshape(pixel_count, channels),
            grad_values[:pixel_count].reshape(pixel_count, channels),
        ],
        axis=1,
    ).astype(jnp.bfloat16)
    grad_pair = jnp.concatenate(
        [
            grad_keys[pixel_count:].reshape(-1, channels),
            grad_values[pixel_count:].reshape(-1, channels),
        ],
        axis=1,
    ).astype(jnp.bfloat16)
    term_out = jnp.einsum("pc,pd->cd", mixed, grad_result, preferred_element_type=jnp.float32)
    term_qkv = jnp.einsum("pc,pk->ck", normed_low, grad_triple, preferred_element_type=jnp.float32)
    term_text = jnp.einsum("tc,tk->ck", text_one, grad_pair, preferred_element_type=jnp.float32)
    big_terms = (term_qkv, term_out, term_text)
    grad_normed = jnp.einsum("pk,ck->pc", grad_triple, qkv_full, preferred_element_type=jnp.float32)
    normed_value, norm_back = jax.vjp(layer_norm, joined, gain_full.astype(jnp.float32))
    grad_joined_norm, term_gain = norm_back(grad_normed)
    return (grad_result.astype(jnp.float32) + grad_joined_norm, term_gain, big_terms)


def every_wide_sum(parts):
    return (
        lax.psum(parts[0].astype(jnp.bfloat16), "wide").astype(jnp.float32),
        lax.psum(parts[1].astype(jnp.bfloat16), "wide").astype(jnp.float32),
        lax.psum(parts[2].astype(jnp.bfloat16), "wide").astype(jnp.float32),
        lax.psum(parts[3].astype(jnp.bfloat16), "wide").astype(jnp.float32),
        lax.psum(parts[4].astype(jnp.bfloat16), "wide").astype(jnp.float32),
        lax.psum(parts[5].astype(jnp.bfloat16), "wide").astype(jnp.float32),
        lax.psum(parts[6].astype(jnp.bfloat16), "wide").astype(jnp.float32),
        lax.psum(parts[7].astype(jnp.bfloat16), "wide").astype(jnp.float32),
        lax.psum(parts[8].astype(jnp.bfloat16), "wide").astype(jnp.float32),
        lax.psum(parts[9].astype(jnp.bfloat16), "wide").astype(jnp.float32),
    )


def plain_body(
    pixels,
    layout,
    noise_group,
    cond_embed,
    text_embed,
    cotangent,
    gn_gain,
    gn_bias,
    conv_in,
    film_weight,
    film_bias,
    conv_out,
    ln_gain,
    qkv_weight,
    out_weight,
    text_weight,
):
    group_total = lax.axis_size("wide")
    onehot_groups = (
        noise_group[:, None] == jnp.arange(group_total, dtype=jnp.int32)[None, :]
    ).astype(jnp.float32)
    counts = lax.psum(jnp.sum(onehot_groups, axis=0), ("wide", "narrow"))
    slot_weights = 1.0 / (group_total * jnp.sum(onehot_groups * counts[None, :], axis=1))
    res_full = (
        lax.all_gather(gn_gain, "narrow", axis=0, tiled=True),
        lax.all_gather(gn_bias, "narrow", axis=0, tiled=True),
        lax.all_gather(conv_in, "narrow", axis=1, tiled=True),
        lax.all_gather(film_weight, "narrow", axis=0, tiled=True),
        lax.all_gather(film_bias, "narrow", axis=0, tiled=True),
        lax.all_gather(conv_out, "narrow", axis=1, tiled=True),
    )
    attn_full = (
        lax.all_gather(ln_gain, "narrow", axis=0, tiled=True),
        lax.all_gather(qkv_weight, "narrow", axis=0, tiled=True),
        lax.all_gather(out_weight, "narrow", axis=0, tiled=True),
        lax.all_gather(text_weight, "narrow", axis=0, tiled=True),
    )
    channels = pixels.shape[2]
    slot_index = 0
    field = pixels[slot_index].astype(jnp.float32)
    region_ids = region_ids_of(layout[slot_index])
    members = (region_ids[:, None] == jnp.arange(4, dtype=jnp.int32)[None, :]).astype(jnp.float32)
    tap_valid = tap_validity(region_ids)
    condition = jax.nn.silu(cond_embed[slot_index].astype(jnp.float32)).astype(jnp.bfloat16)
    front = residual_front(field, members, tap_valid, condition, res_full)
    hidden_two = jnp.dot(
        front[1], res_full[5].reshape(-1, channels), preferred_element_type=jnp.float32
    )
    joined = (field + hidden_two) * inv_root_two
    result, stored = attention_forward(joined, text_embed[slot_index], region_ids, attn_full)
    outputs = [result.astype(jnp.bfloat16)]
    saved = [(field, members, tap_valid, condition, joined, stored)]
    attn_big = tuple((jnp.zeros(full_weight.shape, jnp.float32) for full_weight in attn_full[1:]))
    slot_index = 0
    field, members, tap_valid, condition, joined, stored = saved[slot_index]
    grad_joined, term_gain, big_terms = attention_backward(
        cotangent[slot_index], joined, text_embed[slot_index], stored, attn_full
    )
    joined_grads = [grad_joined]
    gain_sum = slot_weights[slot_index] * term_gain
    attn_big = tuple((slot_weights[slot_index] * fresh for fresh in big_terms))
    grad_ln_gain, grad_qkv_weight, grad_out_weight, grad_text_weight = (
        lax.psum_scatter(
            gain_sum.astype(jnp.bfloat16), "narrow", scatter_dimension=0, tiled=True
        ).astype(jnp.float32),
        lax.psum_scatter(
            attn_big[0].astype(jnp.bfloat16), "narrow", scatter_dimension=0, tiled=True
        ).astype(jnp.float32),
        lax.psum_scatter(
            attn_big[1].astype(jnp.bfloat16), "narrow", scatter_dimension=0, tiled=True
        ).astype(jnp.float32),
        lax.psum_scatter(
            attn_big[2].astype(jnp.bfloat16), "narrow", scatter_dimension=0, tiled=True
        ).astype(jnp.float32),
    )
    res_back = (
        lax.all_gather(gn_gain, "narrow", axis=0, tiled=True),
        lax.all_gather(gn_bias, "narrow", axis=0, tiled=True),
        lax.all_gather(conv_in, "narrow", axis=1, tiled=True),
        lax.all_gather(film_weight, "narrow", axis=0, tiled=True),
        lax.all_gather(film_bias, "narrow", axis=0, tiled=True),
        lax.all_gather(conv_out, "narrow", axis=1, tiled=True),
    )
    conv_first = res_back[2].reshape(-1, channels)
    conv_second = res_back[5].reshape(-1, channels)
    small_sums = (
        jnp.zeros(res_back[0].shape, jnp.float32),
        jnp.zeros(res_back[1].shape, jnp.float32),
        jnp.zeros(res_back[4].shape, jnp.float32),
    )
    res_big = (
        jnp.zeros(res_back[2].shape, jnp.float32),
        jnp.zeros(res_back[3].shape, jnp.float32),
        jnp.zeros(res_back[5].shape, jnp.float32),
    )
    slot_index = 0
    field, members, tap_valid, condition, joined, stored = saved[slot_index]
    grad_joined = joined_grads[slot_index]
    first_cols, second_cols, first_back, mid_back = residual_front(
        field, members, tap_valid, condition, res_back
    )
    grad_two = (grad_joined * inv_root_two).astype(jnp.bfloat16)
    grad_second = fold_back(
        jnp.einsum("pc,kc->pk", grad_two, conv_second, preferred_element_type=jnp.float32),
        tap_valid,
    )
    grad_hidden, grad_film = mid_back(grad_second)
    grad_film_low = grad_film.astype(jnp.bfloat16)
    grad_one = grad_hidden.astype(jnp.bfloat16)
    grad_first = fold_back(
        jnp.einsum("pc,kc->pk", grad_one, conv_first, preferred_element_type=jnp.float32), tap_valid
    )
    grad_field, term_gain, term_bias = first_back(grad_first)
    input_grads = [(grad_joined * inv_root_two + grad_field).astype(jnp.bfloat16)]
    small_terms = (term_gain, term_bias, grad_film_low.astype(jnp.float32))
    small_sums = tuple((slot_weights[slot_index] * fresh for fresh in small_terms))
    term_conv_out = jnp.einsum(
        "pk,pc->kc", second_cols, grad_two, preferred_element_type=jnp.float32
    )
    term_film = jnp.einsum("k,c->kc", condition, grad_film_low, preferred_element_type=jnp.float32)
    term_conv_in = jnp.einsum("pk,pc->kc", first_cols, grad_one, preferred_element_type=jnp.float32)
    big_terms = (
        term_conv_in.reshape(res_back[2].shape),
        term_film,
        term_conv_out.reshape(res_back[5].shape),
    )
    res_big = tuple((slot_weights[slot_index] * fresh for fresh in big_terms))
    grad_gn_gain, grad_gn_bias, grad_conv_in, grad_film_weight, grad_film_bias, grad_conv_out = (
        lax.psum_scatter(
            small_sums[0].astype(jnp.bfloat16), "narrow", scatter_dimension=0, tiled=True
        ).astype(jnp.float32),
        lax.psum_scatter(
            small_sums[1].astype(jnp.bfloat16), "narrow", scatter_dimension=0, tiled=True
        ).astype(jnp.float32),
        lax.psum_scatter(
            res_big[0].astype(jnp.bfloat16), "narrow", scatter_dimension=1, tiled=True
        ).astype(jnp.float32),
        lax.psum_scatter(
            res_big[1].astype(jnp.bfloat16), "narrow", scatter_dimension=0, tiled=True
        ).astype(jnp.float32),
        lax.psum_scatter(
            small_sums[2].astype(jnp.bfloat16), "narrow", scatter_dimension=0, tiled=True
        ).astype(jnp.float32),
        lax.psum_scatter(
            res_big[2].astype(jnp.bfloat16), "narrow", scatter_dimension=1, tiled=True
        ).astype(jnp.float32),
    )
    (
        grad_gn_gain,
        grad_gn_bias,
        grad_conv_in,
        grad_film_weight,
        grad_film_bias,
        grad_conv_out,
        grad_ln_gain,
        grad_qkv_weight,
        grad_out_weight,
        grad_text_weight,
    ) = every_wide_sum(
        (
            grad_gn_gain,
            grad_gn_bias,
            grad_conv_in,
            grad_film_weight,
            grad_film_bias,
            grad_conv_out,
            grad_ln_gain,
            grad_qkv_weight,
            grad_out_weight,
            grad_text_weight,
        )
    )
    return (
        jnp.stack(outputs),
        jnp.stack(input_grads),
        grad_gn_gain,
        grad_gn_bias,
        grad_conv_in,
        grad_film_weight,
        grad_film_bias,
        grad_conv_out,
        grad_ln_gain,
        grad_qkv_weight,
        grad_out_weight,
        grad_text_weight,
    )


CHUNK = 256
HALF_ROWS = 10 * MAP_W
HEAD_DIM = 128


def quadrants(values):
    grid = values.reshape(2, MAP_H // 2, 2, MAP_W // 2, values.shape[-1])
    return [grid[a, :, b] for a in range(2) for b in range(2)]


def rejoin(parts):
    channels = parts[0].shape[-1]
    top = jnp.concatenate(
        [part.reshape(MAP_H // 2, 1, MAP_W // 2, channels) for part in parts[:2]], axis=1
    )
    low = jnp.concatenate(
        [part.reshape(MAP_H // 2, 1, MAP_W // 2, channels) for part in parts[2:]], axis=1
    )
    return jnp.concatenate([top, low], axis=0).reshape(MAP_H * MAP_W, channels)


def region_mean(parts, single, block_ones):
    rows = jnp.concatenate(
        [jnp.sum(part, axis=(0, 1), keepdims=True).reshape(1, -1) for part in parts], axis=0
    )
    rows = jnp.concatenate([rows, rows], axis=0)
    sums = jnp.dot(rows, block_ones, precision=highest, preferred_element_type=jnp.float32)
    quarter_count = (MAP_H * MAP_W // 4) * 32.0
    whole = jnp.sum(sums[:4], axis=0, keepdims=True) * (0.25 / quarter_count)
    return [jnp.where(single, whole, sums[i : i + 1] * (1.0 / quarter_count)) for i in range(4)]


def normalise(parts, single, block_ones):
    means = region_mean(parts, single, block_ones)
    centred = [part - mean[None] for part, mean in zip(parts, means)]
    spread = region_mean([part * part for part in centred], single, block_ones)
    rates = [lax.rsqrt(value + epsilon) for value in spread]
    return [part * rate[None] for part, rate in zip(centred, rates)], rates


def group_ones():
    row = lax.broadcasted_iota(jnp.int32, (CHUNK, CHUNK), 0) // 32
    col = lax.broadcasted_iota(jnp.int32, (CHUNK, CHUNK), 1) // 32
    return (row == col).astype(jnp.float32)


def put_shifts(values, single, taps, lanes):
    shape = values.shape
    pixel = lax.broadcasted_iota(jnp.int32, shape, 0) % MAP_W
    blank = jnp.zeros((MAP_W, shape[1]), jnp.bfloat16)
    for s in range(3):
        if s == 1:
            moved = values
        elif s == 2:
            moved = pltpu.roll(values, MAP_H * MAP_W - 1, 0)
            keep = single(shape) | (pixel != MAP_W // 2 - 1)
            moved = jnp.where((pixel != MAP_W - 1) & keep, moved, 0.0)
        else:
            moved = pltpu.roll(values, 1, 0)
            keep = single(shape) | (pixel != MAP_W // 2)
            moved = jnp.where((pixel != 0) & keep, moved, 0.0)
        low = moved.astype(jnp.bfloat16)
        strip = single((MAP_W, shape[1]))
        taps[s, 0, 0:32, lanes] = blank
        taps[s, 0, 32:288, lanes] = low[0:256]
        taps[s, 0, 288:320, lanes] = jnp.where(strip, moved[256:288], 0.0).astype(jnp.bfloat16)
        taps[s, 1, 0:32, lanes] = jnp.where(strip, moved[224:256], 0.0).astype(jnp.bfloat16)
        taps[s, 1, 32:288, lanes] = low[256:512]
        taps[s, 1, 288:320, lanes] = blank


def tap_rows(taps, col_step, row_step, lanes):
    rows = taps[col_step, :, pl.ds(pl.multiple_of(row_step * MAP_W, MAP_W), 256), lanes]
    return rows.reshape(MAP_H * MAP_W, rows.shape[-1])


def own_first(start, core, width):
    return pl.ds(pl.multiple_of((start + core * 512) % 1024, width), width)


def pair_body(
    pixels,
    layout,
    noise_group,
    cond_embed,
    text_embed,
    cotangent,
    gn_gain,
    gn_bias,
    conv_in,
    film_weight,
    film_bias,
    conv_out,
    ln_gain,
    qkv_weight,
    out_weight,
    text_weight,
):
    f32, bf16 = jnp.float32, jnp.bfloat16
    core = lax.axis_index("narrow")
    text_one = text_embed[0]
    facts = jnp.stack([noise_group[0], layout[0]]).astype(f32)
    facts = jnp.stack([cond_embed[0].astype(f32), jnp.pad(facts, (0, 1022))])
    halves = jnp.stack([gn_gain, gn_bias, ln_gain]).astype(f32)
    big, output, input_grad, small_all, early = run_whole(
        layout,
        pixels[0],
        cotangent[0],
        text_one.T,
        text_one,
        conv_in,
        conv_out,
        film_weight,
        qkv_weight,
        out_weight,
        text_weight,
        jnp.pad(facts, ((0, 6), (0, 0))),
        jnp.pad(halves, ((0, 5), (0, 0))),
        jnp.pad(film_bias.astype(f32)[None], ((0, 7), (0, 0))),
    )
    cond_low = jax.nn.silu(early[:, 0]).astype(bf16)
    grad_film_weight = lax.dot_general(
        half_of(cond_low, core, 1),
        small_all[:, :2].reshape(32, 2048).astype(bf16),
        (((0,), (0,)), ((), ())),
        preferred_element_type=f32,
    )
    small_sum = jnp.sum(small_all, axis=0)
    grad_film_bias = half_of(small_sum[:2].reshape(-1), core, 0)
    grad_gn_gain = half_of(small_sum[2], core, 0)
    grad_gn_bias = half_of(small_sum[3], core, 0)
    grad_ln_gain = half_of(small_sum[4], core, 0)
    tap = (1, 512, 1024)
    conv_shape = (9, 512, 1024)
    return (
        output[None],
        input_grad[None],
        grad_gn_gain,
        grad_gn_bias,
        widen(big, FIRST_IN, conv_shape, tap, 9, lambda k: (k, 0, 0)),
        grad_film_weight,
        grad_film_bias,
        widen(big, FIRST_OUT, conv_shape, tap, 9, lambda k: (k, 0, 0)),
        grad_ln_gain,
        widen(big, FIRST_ATTN, (512, 3072), tap[1:], 3, lambda k: (0, k)),
        widen(big, FIRST_ATTN + 3, (512, 1024), tap[1:], 1, lambda k: (0, 0)),
        widen(big, 0, (2048, 2048), tap[1:], 8, lambda k: (k // 2, k % 2)),
    )


def half_of(value, core, axis):
    size = value.shape[axis] // 2
    return lax.dynamic_slice_in_dim(value, core * size, size, axis)


MESH = pl.DeviceIdType.MESH
CHUNKS = 30
FIRST_OUT, FIRST_ATTN, FIRST_IN = 8, 17, 21
NORMED, GRAD_MIXED, MIXED, TEXT_KEYS, TEXT_VALUES = 12, 16, 20, 24, 25
LAST = (((1,), (1,)), ((), ()))
ROWS = (((0,), (0,)), ((), ()))


def whole_kernel(
    layout,
    field_in, cot_in, text_t, text_in, conv_in, conv_out, film, qkv, out_w, text_w,
    facts_in, halves_in, film_bias_in,
    big, output, input_grad, small_out, early_out,
    in_far, out_far, film_far, qkv_far, out_w_far, text_w_far, cot_far,
    text_src, first_src, second_src, turned, both_own, both_far, rs_land,
    held, total, cross, taps, sources, pair_slots, two_slots, hid_slots, rhs,
    weights, acc, wide_field, extra, field, two_low, hidden_low, hidden_q, pair_q, text_low,
    rows, halves, film_bias, small, early,
    s1s, s1r, s2s, s2r, s3s, s3r, xs, xr, ys, yr, d0s, d0r, d1s, d1r, own_sem,
    pair_s, pair_r, two_s, two_r, hid_s, hid_r, both_s, both_r, rs_s, rs_r,
    small_s, small_r, early_s, early_r,
    in_s, in_r, out_s, out_r, far_s, far_r, text_ws, text_wr,
    src_s, src_r, turn_s, turn_r,
    text_sem, source_sem, rhs_sem, load_sem, weight_sem, keep_sem, turn_sem, both_sem,
):
    f32, bf16 = jnp.float32, jnp.bfloat16
    w = lax.axis_index("wide")
    c = lax.axis_index("narrow")
    me = 2 * w + c
    p = w % 4
    z = w // 4
    wx = w + 1 - 2 * (w % 2)
    wy = w + 2 - 4 * ((w // 2) % 2)
    wd = 4 * z + 3 - p
    wz = w + 4 - 8 * (z % 2)
    wm = (3 - z) * 4 + p
    px = p + 1 - 2 * (p % 2)
    py = p + 2 - 4 * (p // 2)
    pd = 3 - p
    steps = ((wx, px), (wy, py), (wd, pd))
    is_mid = (z == 1) | (z == 2)
    is_end = (z == 0) | (z == 3)
    single = layout[0] == 1

    def remote(src, dst, ss, rs, t):
        return pltpu.make_async_remote_copy(
            src_ref=src, dst_ref=dst, send_sem=ss, recv_sem=rs, device_id=(t, c), device_id_type=MESH
        )

    def across(src, dst, ss, rs):
        return pltpu.make_async_remote_copy(
            src_ref=src, dst_ref=dst, send_sem=ss, recv_sem=rs, device_id=(w, 1 - c),
            device_id_type=MESH,
        )

    def local(src, dst, sem):
        return pltpu.make_async_copy(src, dst, sem)

    loads = [
        local(field_in, field, load_sem.at[0]),
        local(halves_in, halves.at[:, pl.ds(pl.multiple_of(c * 512, 512), 512)], load_sem.at[1]),
        local(film_bias_in, film_bias.at[c], load_sem.at[2]),
        local(facts_in, early.at[me], load_sem.at[3]),
        local(cot_in, two_low, load_sem.at[4]),
    ]
    for copy in loads:
        copy.start()

    bar = pltpu.get_barrier_semaphore()
    for t in (wx, wy, wd, wz):
        pl.semaphore_signal(bar, inc=1, device_id=(t, c), device_id_type=MESH)
    pl.semaphore_signal(bar, inc=1, device_id=(w, 1 - c), device_id_type=MESH)

    @pl.when(is_mid)
    def _():
        pl.semaphore_signal(bar, inc=1, device_id=(wm, c), device_id_type=MESH)
        pl.semaphore_wait(bar, 6)

    @pl.when(is_end)
    def _():
        pl.semaphore_wait(bar, 5)

    def quarter_copies(quarters, slots, ss, rs):
        sends = [
            remote(quarters.at[q], slots.at[2 * (i + 1)], ss.at[i], rs.at[i], t)
            for i, (t, q) in enumerate(steps)
        ]
        sends.append(across(quarters.at[p], slots.at[1], ss.at[3], rs.at[3]))
        passes = [
            across(slots.at[2 * i + 2], slots.at[2 * i + 3], ss.at[4 + i], rs.at[4 + i])
            for i in range(3)
        ]
        return sends, passes

    def start_quarters(quarters, slots, ss, rs, sem):
        sends, _ = quarter_copies(quarters, slots, ss, rs)
        for copy in (sends[2], sends[0], sends[1], sends[3]):
            copy.start()
        local(quarters.at[p], slots.at[0], sem).start()

    def pass_quarters(quarters, slots, ss, rs):
        sends, passes = quarter_copies(quarters, slots, ss, rs)
        for i in range(3):
            sends[i].wait_recv()
            passes[i].start()

    def finish_quarters(quarters, slots, ss, rs, sem):
        sends, passes = quarter_copies(quarters, slots, ss, rs)
        for copy in sends:
            copy.wait_send()
        sends[3].wait_recv()
        for copy in passes:
            copy.wait()
        local(quarters.at[p], slots.at[0], sem).wait()

    def column(q):
        return pl.ds(pl.multiple_of(q * CHUNK, CHUNK), CHUNK)

    def up(k):
        return remote(held.at[k], total.at[k], s1s.at[k], s1r.at[k], wz)

    def over(k):
        return remote(held.at[k], cross.at[k], s2s.at[k], s2r.at[k], wm)

    def down(k):
        return remote(total.at[k], total.at[k], s3s.at[k], s3r.at[k], wz)

    def to_x(k, q):
        return remote(total.at[k], big.at[k, :, column(q)], xs.at[k], xr.at[k], wx)

    def to_y(k, q):
        return remote(total.at[k], big.at[k, :, column(q)], ys.at[k], yr.at[k], wy)

    def on_x(k, q):
        part = big.at[k, pl.ds(0, 256), column(q)]
        return remote(part, part, d0s.at[k], d0r.at[k], wx)

    def on_y(k, q):
        part = big.at[k, pl.ds(256, 256), column(q)]
        return remote(part, part, d1s.at[k], d1r.at[k], wy)

    def own(k):
        return local(total.at[k], big.at[k, :, column(p)], own_sem.at[k])

    def offer(k):
        @pl.when(is_end)
        def _():
            up(k).start()

    def tick(k):
        @pl.when(is_mid & (k < CHUNKS))
        def _():
            up(k).wait_recv()
            held[k] = (held[k].astype(f32) + total[k].astype(f32)).astype(bf16)
            over(k).start()

        kb = k - 1

        @pl.when((kb >= 0) & (kb < CHUNKS))
        def _():
            @pl.when(is_mid)
            def _():
                over(kb).wait_recv()
                total[kb] = (held[kb].astype(f32) + cross[kb].astype(f32)).astype(bf16)
                down(kb).start()

            @pl.when(is_end)
            def _():
                down(kb).wait_recv()

            to_x(kb, p).start()
            to_y(kb, p).start()
            own(kb).start()

        kc = k - 2

        @pl.when((kc >= 0) & (kc < CHUNKS))
        def _():
            to_x(kc, px).wait_recv()
            to_y(kc, py).wait_recv()
            on_x(kc, py).start()
            on_y(kc, px).start()

        kd = k - 3

        @pl.when((kd >= 0) & (kd < CHUNKS))
        def _():
            on_x(kd, pd).wait_recv()
            on_y(kd, pd).wait_recv()

    def in_tap(t):
        return across(conv_in.at[t], in_far.at[t], in_s.at[t], in_r.at[t])

    def out_tap(t):
        return across(conv_out.at[t], out_far.at[t], out_s.at[t], out_r.at[t])

    def text_rows(i):
        part = pl.ds(pl.multiple_of(i * 512, 512), 512)
        return across(text_w.at[part], text_w_far.at[part], text_ws.at[i], text_wr.at[i])

    film_copy = across(film, film_far, far_s.at[0], far_r.at[0])
    qkv_copy = across(qkv, qkv_far, far_s.at[1], far_r.at[1])
    out_w_copy = across(out_w, out_w_far, far_s.at[2], far_r.at[2])
    cot_copy = across(cot_in, cot_far, far_s.at[3], far_r.at[3])
    loads[1].wait()
    loads[2].wait()
    loads[3].wait()
    mine = halves.at[:, pl.ds(pl.multiple_of(c * 512, 512), 512)]
    theirs = halves.at[:, pl.ds(pl.multiple_of(512 - c * 512, 512), 512)]
    halves_copy = across(mine, mine, far_s.at[4], far_r.at[4])
    bias_copy = across(film_bias.at[c], film_bias.at[c], far_s.at[5], far_r.at[5])
    halves_copy.start()
    bias_copy.start()

    def each(count, make):
        def go(i, _):
            make(i).start()
            return 0

        lax.fori_loop(0, count, go, 0)

    each(9, in_tap)
    film_copy.start()

    def doubling(buffer, ss, rs):
        def rows_at(start, count):
            return buffer.at[pl.ds(start, count)]

        def made(r, part):
            if r == 0:
                return across(part, part, ss.at[0], rs.at[0])
            return remote(part, part, ss.at[r], rs.at[r], (None, wx, wy, wz, wm, wz)[r])

        def send(r):
            return made(
                r,
                (
                    rows_at(me, 1),
                    rows_at(2 * w, 2),
                    rows_at(4 * (w // 2), 4),
                    rows_at(8 * z, 8),
                    rows_at(16 * (z // 2), 16),
                    rows_at(16 * (1 - z // 2), 16),
                )[r],
            )

        def arrival(r):
            return made(
                r,
                (
                    rows_at(2 * w + 1 - c, 1),
                    rows_at(2 * wx, 2),
                    rows_at(4 * (wy // 2), 4),
                    rows_at(8 * (wz // 4), 8),
                    rows_at(16 * (wm // 8), 16),
                    rows_at(16 * (1 - z // 2), 16),
                )[r],
            )

        return send, arrival

    early_send, early_arrival = doubling(early, early_s, early_r)
    small_send, small_arrival = doubling(small, small_s, small_r)
    early_send(0).start()

    def plane(n, buffer):
        ss, rs = src_s.at[n], src_r.at[n]
        return (
            remote(buffer.at[0], buffer.at[1], ss.at[0], rs.at[0], wx),
            remote(buffer.at[0], buffer.at[2], ss.at[1], rs.at[1], wy),
            remote(buffer.at[2, 0], buffer.at[3, 0], ss.at[2], rs.at[2], wx),
            remote(buffer.at[1, 1], buffer.at[3, 1], ss.at[3], rs.at[3], wy),
        )

    def plane_first(n, buffer):
        x_copy, y_copy, _, _ = plane(n, buffer)
        x_copy.start()
        y_copy.start()

    def plane_second(n, buffer):
        x_copy, y_copy, on_x_copy, on_y_copy = plane(n, buffer)
        x_copy.wait_recv()
        y_copy.wait_recv()
        on_x_copy.start()
        on_y_copy.start()

    def plane_last(n, buffer):
        x_copy, y_copy, on_x_copy, on_y_copy = plane(n, buffer)
        on_x_copy.wait()
        on_y_copy.wait()
        x_copy.wait_send()
        y_copy.wait_send()

    text_mine = text_t.at[pl.ds(pl.multiple_of(c * 2048, 2048), 2048)]
    text_other = text_t.at[pl.ds(pl.multiple_of(2048 - c * 2048, 2048), 2048)]
    text_turn = (
        local(text_mine, text_src.at[0, 0], turn_sem.at[0]),
        across(text_other, text_src.at[0, 1], turn_s.at[0], turn_r.at[0]),
    )
    for copy in text_turn:
        copy.start()

    def turn(n, own_place, far_place):
        return (
            local(sources.at[2 * (n - 1)], own_place, turn_sem.at[n]),
            across(sources.at[2 * (n - 1) + 1], far_place, turn_s.at[n], turn_r.at[n]),
        )

    first_turn = turn(1, first_src.at[0, 0], first_src.at[0, 1])
    second_turn = turn(2, second_src.at[0, 0], second_src.at[0, 1])
    normed_turn = turn(3, turned.at[0, 0], turned.at[0, 1])
    mixed_turn = turn(4, turned.at[1, 0], turned.at[1, 1])

    def put_turned(n, i, value):
        side = (i // 2 + c) % 2
        sources[2 * (n - 1) + side, pl.ds(pl.multiple_of((i % 2) * CHUNK, CHUNK), CHUNK)] = value.T

    def norm_forward(x, gain, shift, n):
        ones = group_ones()

        def block(i, _):
            lanes = column(i)
            normed, _ = normalise(quadrants(x[:, lanes].astype(f32)), single, ones)
            pre = rejoin(normed) * gain(lanes) + shift(lanes)
            act = pre * jax.nn.sigmoid(pre)
            put_turned(n, i, act.astype(bf16))
            put_shifts(act, lambda shape: single, taps.at[i], slice(None))
            return 0

        lax.fori_loop(0, 4, block, 0)

    def conv_forward(into, side, w_side, arrived):
        def load(t):
            return local(w_side.at[t], weights.at[t % 2, 0], weight_sem.at[t % 2, 0])

        if arrived is not None:
            arrived(0).wait_recv()
        load(0).start()
        half = 2 * ((c + side) % 2)

        def step(t, _):
            @pl.when(t < 8)
            def _():
                if arrived is not None:
                    arrived(t + 1).wait_recv()
                load(t + 1).start()

            load(t).wait()
            part = jnp.concatenate(
                [tap_rows(taps.at[half + i], t % 3, t // 3, slice(None)) for i in range(2)], axis=1
            )
            fresh = jnp.dot(part, weights[t % 2, 0], preferred_element_type=f32)
            if side == 0:

                @pl.when(t == 0)
                def _():
                    into[...] = fresh

                @pl.when(t > 0)
                def _():
                    into[...] += fresh
            else:
                into[...] += fresh
            return 0

        lax.fori_loop(0, 9, step, 0)

    loads[0].wait()
    halves_copy.wait_send()
    across(theirs, theirs, far_s.at[4], far_r.at[4]).wait_recv()
    norm_forward(field, lambda lanes: halves[0:1, lanes], lambda lanes: halves[1:2, lanes], 1)
    for copy in first_turn:
        copy.start()
    for copy in text_turn:
        copy.wait()
    plane_first(0, text_src)
    early_arrival(0).wait_recv()
    early_send(1).start()
    conv_forward(wide_field, 0, conv_in, None)
    conv_forward(wide_field, 1, in_far, in_tap)
    each(9, out_tap)
    qkv_copy.start()
    out_w_copy.start()
    early_arrival(1).wait_recv()
    early_send(2).start()

    film_copy.wait()
    bias_copy.wait_send()
    across(film_bias.at[1 - c], film_bias.at[1 - c], far_s.at[5], far_r.at[5]).wait_recv()
    film_loads = [
        local(
            ref.at[:, pl.ds(1024 * b, 1024)], weights.at[side, b], weight_sem.at[side, b]
        )
        for side, ref in enumerate((film, film_far))
        for b in range(2)
    ]
    for copy in film_loads:
        copy.start()
    for copy in film_loads:
        copy.wait()
    cond = early[pl.ds(me, 1), 0:1].reshape(1, 1024)
    early_row = early.at[me]
    for b in range(2):
        value = film_bias[b, 0:1]
        for side in range(2):
            lanes = pl.ds(pl.multiple_of(((c + side) % 2) * 512, 512), 512)
            part = early_row[0:1, lanes]
            part = jnp.broadcast_to(part * jax.nn.sigmoid(part), (16, 512)).astype(bf16)
            value += jnp.dot(part, weights[side, b], preferred_element_type=f32)[0:1]
        rows[b : b + 1] = value + (1.0 - b)
    rows[2:3] = halves[0:1]
    rows[3:4] = halves[1:2]

    norm_forward(wide_field, lambda lanes: rows[0:1, lanes], lambda lanes: rows[1:2, lanes], 2)
    for copy in second_turn:
        copy.start()
    for copy in second_turn:
        copy.wait()
    plane_first(1, second_src)
    plane_second(0, text_src)
    early_arrival(2).wait_recv()
    early_send(3).start()
    conv_forward(acc, 0, conv_out, None)
    each(4, text_rows)
    cot_copy.start()
    conv_forward(acc, 1, out_far, out_tap)

    def by_rows(body):
        def go(i, _):
            body(pl.ds(pl.multiple_of(i * 128, 128), 128))
            return 0

        lax.fori_loop(0, 4, go, 0)

    def layer_norm_rows(part):
        joined = (field[part].astype(f32) + acc[part]) * inv_root_two
        acc[part] = joined
        centre = joined - jnp.mean(joined, axis=1, keepdims=True)
        rate = lax.rsqrt(jnp.mean(centre * centre, axis=1, keepdims=True) + epsilon)
        normed = (centre * rate * halves[2:3]).astype(bf16)
        for i in range(4):
            held[NORMED + i, part] = normed[:, i * CHUNK : (i + 1) * CHUNK]

    by_rows(layer_norm_rows)
    early_arrival(3).wait_recv()

    @pl.when(is_mid)
    def _():
        early_send(4).start()

    def turn_block(n, base):
        def go(i, _):
            put_turned(n, i, held[base + i])
            return 0

        lax.fori_loop(0, 4, go, 0)

    turn_block(3, NORMED)
    for copy in normed_turn:
        copy.start()

    def sides(base, side):
        half = base + 2 * ((c + side) % 2)
        return jnp.concatenate([held[half], held[half + 1]], axis=1)

    qkv_copy.wait()

    def qkv_loads(m):
        lanes = pl.ds(pl.multiple_of(m * 1024, 1024), 1024)
        return [
            local(ref.at[:, lanes], weights.at[m % 2, side], weight_sem.at[m % 2, side])
            for side, ref in enumerate((qkv, qkv_far))
        ]

    def qkv_pass(body):
        for copy in qkv_loads(0):
            copy.start()

        def step(m, _):
            @pl.when(m < 2)
            def _():
                for copy in qkv_loads(m + 1):
                    copy.start()

            for copy in qkv_loads(m):
                copy.wait()
            body(m)
            return 0

        lax.fori_loop(0, 3, step, 0)

    def project(m):
        value = jnp.dot(sides(NORMED, 0), weights[m % 2, 0], preferred_element_type=f32)
        value += jnp.dot(sides(NORMED, 1), weights[m % 2, 1], preferred_element_type=f32)
        value = value.astype(bf16)
        for i in range(4):
            held[4 * m + i] = value[:, i * CHUNK : (i + 1) * CHUNK]

    qkv_pass(project)

    out_w_copy.wait()
    out_w_loads = [
        local(ref, weights.at[1, side], weight_sem.at[1, side])
        for side, ref in enumerate((out_w, out_w_far))
    ]
    for copy in out_w_loads:
        copy.start()
    loads[4].wait()
    for copy in out_w_loads:
        copy.wait()
    for side in range(2):
        value = lax.dot_general(two_low[...], weights[1, side], LAST, preferred_element_type=f32)
        value = value.astype(bf16)
        half = GRAD_MIXED + 2 * ((c + side) % 2)
        held[half] = value[:, :CHUNK]
        held[half + 1] = value[:, CHUNK:]

    def text_w_loads(s):
        side = s // 4
        part = pl.ds(pl.multiple_of((s % 4) * 512, 512), 512)
        lanes = pl.ds(pl.multiple_of(((c + side) % 2) * 2048 + (s % 4) * 512, 512), 512)
        slot = s % 2
        return (
            [
                local(
                    ref.at[part, pl.ds(1024 * b, 1024)], weights.at[slot, b], weight_sem.at[slot, b]
                )
                for ref in (text_w, text_w_far)
                for b in range(2)
            ],
            local(text_in.at[:, lanes], text_low.at[slot], turn_sem.at[5 + slot]),
        )

    def start_text(s):
        weight_copies, text_copy = text_w_loads(s)
        text_copy.start()

        @pl.when(s < 4)
        def _():
            for copy in weight_copies[:2]:
                copy.start()

        @pl.when(s >= 4)
        def _():
            text_rows(s - 4).wait_recv()
            for copy in weight_copies[2:]:
                copy.start()

    start_text(0)
    extra[0:256] = jnp.zeros((256, 1024), f32)

    def text_pair_step(s, _):
        @pl.when(s < 7)
        def _():
            start_text(s + 1)

        weight_copies, text_copy = text_w_loads(s)
        text_copy.wait()
        for b in range(2):
            weight_copies[b].wait()
            extra[128 * b : 128 * b + 128] += jnp.dot(
                text_low[s % 2], weights[s % 2, b], preferred_element_type=f32
            )
        return 0

    lax.fori_loop(0, 8, text_pair_step, 0)
    for i in range(4):
        lanes = slice(i * CHUNK, (i + 1) * CHUNK)
        held[TEXT_KEYS, 128 * i : 128 * i + 128] = extra[0:128, lanes].astype(bf16)
        held[TEXT_VALUES, 128 * i : 128 * i + 128] = extra[128:256, lanes].astype(bf16)

    @pl.when(is_mid)
    def _():
        early_arrival(4).wait_recv()
        early_send(5).start()

    @pl.when(is_end)
    def _():
        early_arrival(5).wait_recv()

    groups = early[:, 1:2, 0:1]

    def image_weight(row):
        alike = (groups == early[pl.ds(row, 1), 1:2, 0:1]).astype(f32)
        return (1.0 / (16.0 * jnp.sum(alike, axis=0, keepdims=True))).reshape(1, 1)

    weight = image_weight(me)
    far_weight = image_weight(2 * w + 1 - c)

    def layout_of(i):
        chip = (w, wx, wy, wd)[i // 2]
        row = 2 * chip + (c if i % 2 == 0 else 1 - c)
        flag = early[pl.ds(row, 1), 1:2, 1:2].reshape(1, 1)
        return lambda shape: jnp.broadcast_to(flag, shape) == 1.0

    scale = HEAD_DIM ** (-0.5)

    def region(axis, shape):
        position = lax.broadcasted_iota(jnp.int32, shape, axis)
        return 2 * (position // 256) + (position % MAP_W) // (MAP_W // 2)

    def attention(j, _):
        for h in range(2):
            lanes = slice(h * HEAD_DIM, (h + 1) * HEAD_DIM)
            q, key, value = held[j, :, lanes], held[4 + j, :, lanes], held[8 + j, :, lanes]
            text_part = pl.ds(pl.multiple_of(128 * j, 128), 128)
            text_key, text_value = held[TEXT_KEYS, text_part, lanes], held[TEXT_VALUES, text_part, lanes]
            grad = held[GRAD_MIXED + j, :, lanes]
            keys = jnp.concatenate([key, text_key], axis=0)
            values = jnp.concatenate([value, text_value], axis=0)
            scores = lax.dot_general(q, keys, LAST, preferred_element_type=f32) * scale
            shape = (512, 640)
            allowed = (region(0, shape) == region(1, shape)) | (
                lax.broadcasted_iota(jnp.int32, shape, 1) >= 512
            )
            scores = jnp.where(single | allowed, scores, masked_score)
            exponent = jnp.exp(scores - jnp.max(scores, axis=1, keepdims=True))
            probs = exponent / jnp.sum(exponent, axis=1, keepdims=True)
            probs_low = probs.astype(bf16)
            held[MIXED + j, :, lanes] = jnp.dot(
                probs_low, values, preferred_element_type=f32
            ).astype(bf16)
            grad_probs = lax.dot_general(grad, values, LAST, preferred_element_type=f32)
            grad_values = lax.dot_general(probs_low, grad, ROWS, preferred_element_type=f32)
            inner = jnp.sum(probs * grad_probs, axis=1, keepdims=True)
            grad_scores = (probs * (grad_probs - inner)).astype(bf16)
            grad_q = jnp.dot(grad_scores, keys, preferred_element_type=f32) * scale
            grad_keys = lax.dot_general(grad_scores, q, ROWS, preferred_element_type=f32) * scale
            held[j, :, lanes] = grad_q.astype(bf16)
            held[4 + j, :, lanes] = grad_keys[:512].astype(bf16)
            held[8 + j, :, lanes] = grad_values[:512].astype(bf16)
            pair_q[j, :, lanes] = (grad_keys[512:] * weight).astype(bf16)
            pair_q[j, :, CHUNK + h * HEAD_DIM : CHUNK + (h + 1) * HEAD_DIM] = (
                grad_values[512:] * weight
            ).astype(bf16)
        return 0

    lax.fori_loop(0, 4, attention, 0)
    start_quarters(pair_q, pair_slots, pair_s, pair_r, keep_sem.at[0])
    turn_block(4, MIXED)
    for copy in mixed_turn:
        copy.start()

    def both_place(ref, i):
        return ref.at[:, pl.ds(pl.multiple_of(i * CHUNK, CHUNK), CHUNK)]

    def both_keep(i):
        return local(held.at[i], both_place(both_own, i), both_sem.at[i])

    def both_send(i):
        return across(held.at[i], both_place(both_far, i), both_s.at[i], both_r.at[i])

    each(12, both_send)
    each(12, both_keep)

    def project_back(m):
        left = jnp.concatenate([held[4 * m + i] for i in range(4)], axis=1)
        for side in range(2):
            lanes = pl.ds(pl.multiple_of(((c + side) % 2) * 512, 512), 512)
            fresh = lax.dot_general(left, weights[m % 2, side], LAST, preferred_element_type=f32)

            @pl.when(m == 0)
            def _():
                extra[:, lanes] = fresh

            @pl.when(m > 0)
            def _():
                extra[:, lanes] += fresh

    qkv_pass(project_back)
    rows[4:8] = jnp.zeros((4, 1024), f32)

    def layer_norm_back(part):
        joined = acc[part]
        centre = joined - jnp.mean(joined, axis=1, keepdims=True)
        rate = lax.rsqrt(jnp.mean(centre * centre, axis=1, keepdims=True) + epsilon)
        y = centre * rate
        grad = extra[part]
        rows[4:5] += jnp.sum(grad * y, axis=0, keepdims=True)
        grad = grad * halves[2:3]
        mean = jnp.mean(grad, axis=1, keepdims=True)
        slope = jnp.mean(grad * y, axis=1, keepdims=True)
        grad = two_low[part].astype(f32) + (grad - mean - y * slope) * rate
        extra[part] = grad
        two = grad * inv_root_two
        two_low[part] = two.astype(bf16)
        two = (two * weight).astype(bf16)
        for i in range(4):
            held[NORMED + i, part] = two[:, i * CHUNK : (i + 1) * CHUNK]

    by_rows(layer_norm_back)
    two_q = held.at[pl.ds(NORMED, 4)]
    start_quarters(two_q, two_slots, two_s, two_r, keep_sem.at[1])
    pass_quarters(pair_q, pair_slots, pair_s, pair_r)

    out_w_loads = [
        local(ref, weights.at[1, side], weight_sem.at[1, side])
        for side, ref in enumerate((out_w, out_w_far))
    ]
    for copy in out_w_loads:
        copy.start()
    for copy in out_w_loads:
        copy.wait()
    value = jnp.dot(sides(MIXED, 0), weights[1, 0], preferred_element_type=f32)
    value += jnp.dot(sides(MIXED, 1), weights[1, 1], preferred_element_type=f32)
    hidden_low[...] = (acc[...] + value).astype(bf16)
    output_keep = local(hidden_low, output, keep_sem.at[6])
    output_keep.start()

    plane_second(1, second_src)
    plane_last(0, text_src)
    for copy in first_turn:
        copy.wait()
    plane_first(2, first_src)
    finish_quarters(pair_q, pair_slots, pair_s, pair_r, keep_sem.at[0])

    def both_done(i, _):
        both_send(i).wait()
        both_keep(i).wait()
        return 0

    lax.fori_loop(0, 12, both_done, 0)
    for copy in normed_turn + mixed_turn:
        copy.wait()

    def text_loads(i):
        slot = 2 * (i % 2)
        rows_i = pl.ds(pl.multiple_of(i * 512, 512), 512)
        return [
            local(
                text_src.at[j, e, rows_i],
                sources.at[slot + j // 2, :, pl.ds(TEXT_LEN * (2 * (j % 2) + e), TEXT_LEN)],
                text_sem.at[i % 2, 2 * j + e],
            )
            for j in range(4)
            for e in range(2)
        ]

    for copy in text_loads(0):
        copy.start()
    turned_loads = [
        local(
            turned.at[kind, side],
            weights.at[0, kind, :, pl.ds(512 * side, 512)],
            weight_sem.at[kind, side],
        )
        for kind in range(2)
        for side in range(2)
    ]
    for copy in turned_loads:
        copy.start()

    def text_step(i, _):
        @pl.when(i < 3)
        def _():
            for copy in text_loads(i + 1):
                copy.start()

        for copy in text_loads(i):
            copy.wait()
        slot = 2 * (i % 2)
        right = pair_slots[...].reshape(8 * TEXT_LEN, 2 * CHUNK)
        value = jnp.dot(sources[slot], right[:512], preferred_element_type=f32)
        value += jnp.dot(sources[slot + 1], right[512:], preferred_element_type=f32)
        value = value.astype(bf16)
        held[2 * i] = value[:, :CHUNK]
        held[2 * i + 1] = value[:, CHUNK:]
        offer(2 * i)
        offer(2 * i + 1)
        return 0

    lax.fori_loop(0, 4, text_step, 0)

    def source_loads(parts):
        return [
            local(parts.at[j, e], sources.at[2 * j + e], source_sem.at[2 * j + e])
            for j in range(4)
            for e in range(2)
        ]


    cot_copy.wait()
    for copy in turned_loads:
        copy.wait()

    class rhs_loads:
        def __init__(self, q, j, slot):
            self.q, self.j, self.slot = q, j, slot

        def copies(self, pair, col):
            return [
                local(
                    ref.at[:, col], rhs.at[self.slot, pl.ds(512 * i, 512)], rhs_sem.at[self.slot, i]
                )
                for i, ref in enumerate(pair)
            ]

        def start(self):
            @pl.when(self.j < 3)
            def _():
                col = pl.ds(pl.multiple_of(self.j * 1024 + self.q * CHUNK, CHUNK), CHUNK)
                for copy in self.copies((both_own, both_far), col):
                    copy.start()

            @pl.when(self.j == 3)
            def _():
                for copy in self.copies((cot_in, cot_far), column(self.q)):
                    copy.start()

        def wait(self):
            for copy in self.copies((cot_in, cot_far), column(self.q)):
                copy.wait()

    staged = (hidden_q, held, held, held)
    staged_base = (0, FIRST_IN, FIRST_IN + 4, FIRST_ATTN)

    def rs_copy(m, j):
        return remote(
            staged[m].at[staged_base[m] + j], rs_land.at[m, j], rs_s.at[m, j], rs_r.at[m, j], steps[m][0]
        )

    order = (2, 0, 1, 3)
    quarter_of = (px, py, pd, p)
    rhs_loads(quarter_of[2], jnp.int32(0), 0).start()
    for place, m in enumerate(order):

        def attn_step(j, _, m=m, place=place):
            slot = j % 2

            @pl.when(j < 3)
            def _():
                rhs_loads(quarter_of[m], j + 1, 1 - slot).start()

            if place < 3:

                @pl.when(j == 3)
                def _():
                    rhs_loads(quarter_of[order[place + 1]], jnp.int32(0), 1 - slot).start()

            rhs_loads(quarter_of[m], j, slot).wait()
            left = weights[0, j // 3]
            value = weight * jnp.dot(
                left[:, :512], rhs[slot, :512], preferred_element_type=f32
            ) + far_weight * jnp.dot(left[:, 512:], rhs[slot, 512:], preferred_element_type=f32)
            staged[m][staged_base[m] + j] = value.astype(bf16)
            if m < 3:
                rs_copy(m, j).start()
            return 0

        lax.fori_loop(0, 4, attn_step, 0)
        if place == 1:
            pass_quarters(two_q, two_slots, two_s, two_r)
            tick(0)
        if place == 3:
            tick(1)

    def conv_term_taps(slots):
        for i in range(8):
            put_shifts(slots[i].astype(f32), layout_of(i), taps.at[i], slice(None))

    def conv_term_loop(base, first_tick):
        def step(t, _):
            value = jnp.zeros((512, CHUNK), f32)
            for i in range(8):
                part = tap_rows(taps.at[i], 2 - t % 3, 2 - t // 3, slice(None))
                value += jnp.dot(sources[i], part, preferred_element_type=f32)
            held[base + t] = value.astype(bf16)
            offer(base + t)

            @pl.when(t % 3 == 2)
            def _():
                tick(first_tick + t // 3)

            return 0

        lax.fori_loop(0, 9, step, 0)

    finish_quarters(two_q, two_slots, two_s, two_r, keep_sem.at[1])
    conv_term_taps(two_slots)
    plane_last(1, second_src)
    second_loads = source_loads(second_src)
    for copy in second_loads:
        copy.start()
    for copy in second_loads:
        copy.wait()
    conv_term_loop(FIRST_OUT, 2)

    def conv_back(grad, w_own, w_far, first_tick):
        def weight_loads(t):
            slot = t % 2
            return (
                local(w_own.at[t], weights.at[slot, 0], weight_sem.at[slot, 0]),
                local(w_far.at[t], weights.at[slot, 1], weight_sem.at[slot, 1]),
            )

        for copy in weight_loads(0):
            copy.start()
        for i in range(4):
            put_shifts(
                grad[:, i * CHUNK : (i + 1) * CHUNK].astype(f32),
                lambda shape: single,
                taps.at[i],
                slice(None),
            )
        acc[...] = jnp.zeros((512, 1024), f32)

        def step(t, _):
            @pl.when(t < 8)
            def _():
                for copy in weight_loads(t + 1):
                    copy.start()

            for copy in weight_loads(t):
                copy.wait()
            part = jnp.concatenate(
                [tap_rows(taps.at[i], 2 - t % 3, 2 - t // 3, slice(None)) for i in range(4)], axis=1
            )
            for side in range(2):
                acc[:, side * 512 : side * 512 + 512] += lax.dot_general(
                    part, weights[t % 2, side], LAST, preferred_element_type=f32
                )

            @pl.when(t % 3 == 2)
            def _():
                tick(first_tick + t // 3)

            return 0

        lax.fori_loop(0, 9, step, 0)

    def norm_back(x, at, put):
        ones = group_ones()

        def block(i, _):
            lanes = column(i)
            parts = quadrants(x[:, lanes].astype(f32))
            normed, rates = normalise(parts, single, ones)
            gains = rows[at : at + 1, lanes]
            shift = rows[at + 1 : at + 2, lanes]
            pre = [part * gains[None] + shift[None] for part in normed]
            grads = quadrants(acc[:, own_first(i * CHUNK, c, CHUNK)])
            sig = [jax.nn.sigmoid(part) for part in pre]
            grads = [g * s * (1.0 + v * (1.0 - s)) for g, s, v in zip(grads, sig, pre)]
            small[pl.ds(2 * w + c, 1), at : at + 1, lanes] = sum(
                jnp.sum(g * n, axis=(0, 1), keepdims=True) for g, n in zip(grads, normed)
            )
            small[pl.ds(2 * w + c, 1), at + 1 : at + 2, lanes] = sum(
                jnp.sum(g, axis=(0, 1), keepdims=True) for g in grads
            )
            grads = [g * gains[None] for g in grads]
            mean = region_mean(grads, single, ones)
            slope = region_mean([g * n for g, n in zip(grads, normed)], single, ones)
            put(
                i,
                lanes,
                rejoin(
                    [
                        r[None] * (g - m[None] - n * s[None])
                        for r, g, m, n, s in zip(rates, grads, mean, normed, slope)
                    ]
                ),
            )
            return 0

        lax.fori_loop(0, 4, block, 0)

    conv_back(two_low, conv_out, out_far, 5)
    output_keep.wait()

    for m in range(3):
        for j in range(4):
            rs_copy(m, j).wait_send()

    def put_hidden(i, lanes, value):
        hidden_low[:, lanes] = value.astype(bf16)
        hidden_q[i] = (value * weight).astype(bf16)

    norm_back(wide_field, 0, put_hidden)
    start_quarters(hidden_q, hid_slots, hid_s, hid_r, keep_sem.at[2])

    for m in range(3):
        for j in range(4):
            rs_copy(m, j).wait_recv()

    def attn_sum(j, _):
        k = FIRST_ATTN + j
        value = held[k].astype(f32)
        fresh = [
            local(
                rs_land.at[m, j], rhs.at[m // 2, pl.ds(512 * (m % 2), 512)], rhs_sem.at[m // 2, m % 2]
            )
            for m in range(3)
        ]
        for copy in fresh:
            copy.start()
        for copy in fresh:
            copy.wait()
        for m in range(3):
            value += rhs[m // 2, 512 * (m % 2) : 512 * (m % 2) + 512].astype(f32)
        held[k] = value.astype(bf16)
        offer(k)
        return 0

    lax.fori_loop(0, 4, attn_sum, 0)
    tick(8)

    plane_second(2, first_src)
    conv_back(hidden_low, conv_in, in_far, 9)

    def put_input(i, lanes, value):
        two_low[:, lanes] = (value + extra[:, lanes] * inv_root_two).astype(bf16)

    norm_back(field, 2, put_input)
    keep = local(two_low, input_grad, keep_sem.at[4])
    keep.start()
    small[pl.ds(me, 1), 4:8] = rows[4:8][None]
    small[pl.ds(me, 1)] = small[pl.ds(me, 1)] * weight[None]
    pass_quarters(hidden_q, hid_slots, hid_s, hid_r)
    tick(12)
    finish_quarters(hidden_q, hid_slots, hid_s, hid_r, keep_sem.at[2])
    conv_term_taps(hid_slots)
    plane_last(2, first_src)
    first_loads = source_loads(first_src)
    for copy in first_loads:
        copy.start()
    for copy in first_loads:
        copy.wait()

    small_send(0).start()
    conv_term_loop(FIRST_IN, 13)
    for r in range(4):
        small_arrival(r).wait_recv()
        if r < 3:
            small_send(r + 1).start()
        tick(16 + r)

    @pl.when(is_mid)
    def _():
        small_send(4).start()
        small_arrival(4).wait_recv()
        small_send(5).start()

    def rest(k, _):
        tick(k)
        return 0

    lax.fori_loop(20, CHUNKS + 3, rest, 0)

    @pl.when(is_end)
    def _():
        small_arrival(5).wait_recv()

    for r in range(4):
        small_send(r).wait_send()

    @pl.when(is_mid)
    def _():
        small_send(4).wait_send()
        small_send(5).wait_send()

    small_keep = local(small, small_out, keep_sem.at[5])
    small_keep.start()
    early_keep = local(early, early_out, keep_sem.at[3])
    early_keep.start()
    for r in range(4):
        early_send(r).wait_send()

    @pl.when(is_mid)
    def _():
        early_send(4).wait_send()
        early_send(5).wait_send()

    def sent(i, _):
        in_tap(i).wait_send()
        out_tap(i).wait_send()
        return 0

    lax.fori_loop(0, 9, sent, 0)

    def text_sent(i, _):
        text_rows(i).wait_send()
        return 0

    lax.fori_loop(0, 4, text_sent, 0)

    def finish(k, _):
        @pl.when(is_end)
        def _():
            up(k).wait_send()

        @pl.when(is_mid)
        def _():
            over(k).wait_send()
            down(k).wait_send()

        to_x(k, p).wait_send()
        to_y(k, p).wait_send()
        on_x(k, py).wait_send()
        on_y(k, px).wait_send()
        own(k).wait()
        return 0

    lax.fori_loop(0, CHUNKS, finish, 0)
    keep.wait()
    small_keep.wait()
    early_keep.wait()


def run_whole(layout, *operands):
    bf16, f32 = jnp.bfloat16, jnp.float32
    any_spec = pl.BlockSpec(memory_space=pl.ANY)
    dma = pltpu.SemaphoreType.DMA
    chunks = pltpu.VMEM((CHUNKS, 512, CHUNK), bf16)
    map_low = pltpu.VMEM((512, 1024), bf16)
    map_full = pltpu.VMEM((512, 1024), f32)
    slots = pltpu.VMEM((8, 512, CHUNK), bf16)
    table = pltpu.VMEM((32, 8, 1024), f32)
    low_shapes = (
        (9, 512, 1024), (9, 512, 1024), (512, 2048), (512, 3072), (512, 1024), (2048, 2048),
        (512, 1024), (4, 2, 2048, TEXT_LEN), (4, 2, 512, 512), (4, 2, 512, 512), (2, 2, 512, 512),
        (512, 3072), (512, 3072), (3, 4, 512, CHUNK),
    )
    full_rows = jax.ShapeDtypeStruct((32, 8, 1024), f32)
    field = jax.ShapeDtypeStruct((512, 1024), bf16)
    outs = (jax.ShapeDtypeStruct((CHUNKS, 512, 1024), bf16), field, field, full_rows, full_rows)
    outs += tuple(jax.ShapeDtypeStruct(shape, bf16) for shape in low_shapes)
    found = pl.pallas_call(
        whole_kernel,
        out_shape=outs,
        in_specs=[pl.BlockSpec(memory_space=pltpu.SMEM)] + [any_spec] * len(operands),
        out_specs=[any_spec] * len(outs),
        scratch_shapes=[
            chunks, chunks, chunks,
            pltpu.VMEM((8, 3, 2, HALF_ROWS, CHUNK), bf16),
            pltpu.VMEM((8, 512, 512), bf16),
            pltpu.VMEM((8, TEXT_LEN, 2 * CHUNK), bf16),
            slots, slots,
            pltpu.VMEM((2, 1024, CHUNK), bf16),
            pltpu.VMEM((2, 2, 512, 1024), bf16),
            map_full, map_full, map_full, map_low, map_low, map_low,
            pltpu.VMEM((4, 512, CHUNK), bf16),
            pltpu.VMEM((4, TEXT_LEN, 2 * CHUNK), bf16),
            pltpu.VMEM((2, TEXT_LEN, 512), bf16),
            pltpu.VMEM((8, 1024), f32),
            pltpu.VMEM((8, 1024), f32),
            pltpu.VMEM((2, 8, 1024), f32),
            table, table,
        ]
        + [dma((CHUNKS,))] * 15
        + [dma((7,))] * 6
        + [dma((12,))] * 2 + [dma((3, 4))] * 2 + [dma((6,))] * 4
        + [dma((9,))] * 4 + [dma((6,))] * 2 + [dma((4,))] * 2
        + [dma((3, 4))] * 2 + [dma((5,))] * 2
        + [dma((2, 8)), dma((8,)), dma((2, 2)), dma((5,)), dma((2, 2)), dma((7,)), dma((7,)), dma((12,))],
        compiler_params=pltpu.CompilerParams(
            collective_id=0, has_side_effects=True, vmem_limit_bytes=63 << 20
        ),
        name="whole_step",
    )(layout, *operands)
    return found[:5]


def widen_kernel(low, out):
    out[...] = low[...].reshape(out.shape).astype(jnp.float32)


def widen(big, first, shape, block, count, where):
    return pl.pallas_call(
        widen_kernel,
        out_shape=jax.ShapeDtypeStruct(shape, jnp.float32),
        grid=(count,),
        in_specs=[pl.BlockSpec((1, 512, 1024), lambda k: (first + k, 0, 0))],
        out_specs=pl.BlockSpec(block, where),
        name="widen",
    )(big)


def solution(mesh):
    fits = mesh.shape["wide"] == 16 and mesh.shape["narrow"] == 2
    body = pair_body if fits else plain_body
    placed = (
        P(("wide", "narrow"), None, None),
        P(("wide", "narrow")),
        P(("wide", "narrow")),
        P(("wide", "narrow"), None),
        P(("wide", "narrow"), None, None),
        P(("wide", "narrow"), None, None),
        P("narrow"),
        P("narrow"),
        P(None, "narrow", None),
        P("narrow", None),
        P("narrow"),
        P(None, "narrow", None),
        P("narrow"),
        P("narrow", None),
        P("narrow", None),
        P("narrow", None),
    )
    return jax.shard_map(
        body,
        mesh=mesh,
        in_specs=placed,
        out_specs=(
            P(("wide", "narrow"), None, None),
            P(("wide", "narrow"), None, None),
            P("narrow"),
            P("narrow"),
            P(None, "narrow", None),
            P("narrow", None),
            P("narrow"),
            P(None, "narrow", None),
            P("narrow"),
            P("narrow", None),
            P("narrow", None),
            P("narrow", None),
        ),
        check_vma=False,
    )
```
